256 devices in a mesh: gx: 64 (over z, y, core), gy: 4 (over x).
Axes of the slice: x: 4, y: 4, z: 8, core: 2. Of those that a mesh axis runs over, the one named last changes fastest.
Arguments:
- body_load: float32 [64, 4, 6, 512], P('gx', 'gy'), may hold values from -54 to 54
- proximal: float32 [64, 4, 6, 512], P('gx', 'gy'), may hold values from 1 to 8
- contact_blocks: float32 [64, 4, 6, 12, 2048], P('gx', 'gy'), may hold values from -1.75 to 1.75
- slacks: float32 [64, 4, 6, 2048], P('gx', 'gy'), may hold values from 0.5 to 5
- dual_rows: float32 [64, 4, 6, 2048], P('gx', 'gy'), may hold values from 0.1 to 2
- first_body: int32 [64, 4, 2048], P('gx', 'gy'), may hold values from 0 to 511
- second_body: int32 [64, 4, 2048], P('gx', 'gy'), may hold values from 0 to 767
- border_bodies: int32 [64, 4, 8, 32], P('gx', 'gy'), may hold values from 0 to 511
Outputs:
- velocity_step: float32 [64, 4, 6, 512], P('gx', 'gy')
- residual: float32 [64, 4, 6, 512], P('gx', 'gy')
The draws below stay inside these ranges and needn't reach their ends.
All inputs are finite; a program needn't handle non-finite values.
Results may differ from the reference program's by a relative error of at most 0.0003.
Values sent between devices are 32-bit elements; how exact they have to be, the bound alone decides.
A program may use at most 128 MiB of HBM per device.

```python
import math
import jax
import jax.numpy as jnp
from jax import lax

BODY_DEV = 512
SEND = 32
CONTACTS_DEV = 2048
ITERS = 4
N_GX = 64
N_GY = 4


def draw_body_load(key, part):
    key = jax.random.fold_in(key, 17)
    along_ramp = 1.0 + 2.0 * jnp.arange(N_GX, dtype=jnp.float32)[:, None, None, None] / max(N_GX - 1, 1)
    base_values = jnp.clip(jax.random.normal(key, (N_GX, N_GY, 6, BODY_DEV), jnp.float32), -6.0, 6.0)
    return (3.0 * along_ramp * base_values).astype(jnp.float32)


def touch_ends(result, stream_key, low, largest):
    longest = result.shape.index(max(result.shape))
    spots = []
    for shift in (0, 1):
        where = [jax.random.randint(jax.random.fold_in(stream_key, axis), (), 0, length) for axis, length in enumerate(result.shape)]
        where[longest] = (where[longest] + shift) % result.shape[longest]
        spots.append(tuple(where))
    return result.at[spots[0]].set(low).at[spots[1]].set(largest)


def level_of(own_key, extent, cuts, least, largest):
    gain, own = 1.0, jax.random.fold_in(own_key, 6)
    for dim, parts in cuts:
        heights = jnp.exp(jax.random.uniform(jax.random.fold_in(own, dim), (parts,), jnp.float32, least / len(cuts), largest / len(cuts)))
        gain = gain * jnp.repeat(heights, extent[dim] // parts).reshape([-1 if axis == dim else 1 for axis in range(len(extent))])
    return gain


def centred(rng, dims, width, most, cuts=(), held_as=jnp.bfloat16):
    loudness = level_of(rng, dims, cuts, -0.22, 0.18) if cuts else 1.0
    result = jax.random.normal(rng, dims, jnp.float32) * width * loudness
    return jnp.minimum(jnp.maximum(result, -most), most).astype(held_as)


def setup_inputs(seed: int = 0) -> dict:
    keys = jax.random.split(jax.random.key(seed), 9)
    body_load = draw_body_load(jax.random.fold_in(keys[8], 71), 0)
    proximal = jnp.clip(jnp.exp(math.log(8.0) - 2.0794415 * jax.random.uniform(keys[1], (N_GX, N_GY, 6, BODY_DEV), jnp.float32) ** level_of(keys[1], (N_GX, N_GY, 6, BODY_DEV), ((0, 64), (1, 4)), -0.2, 0.2)), 1.0, 8.0)
    contact_blocks = centred(keys[2], (N_GX, N_GY, 6, 12, CONTACTS_DEV), 12 ** -0.5, 1.75, ((0, 64), (1, 4)), jnp.float32)
    slacks = jnp.clip(jnp.exp(math.log(5.0) - 2.3025851 * jax.random.uniform(keys[3], (N_GX, N_GY, 6, CONTACTS_DEV), jnp.float32) ** level_of(keys[3], (N_GX, N_GY, 6, CONTACTS_DEV), ((0, 64), (1, 4)), -0.2, 0.2)), 0.5, 5.0)
    dual_rows = jnp.clip(jnp.exp(math.log(2.0) - 2.9957323 * jax.random.uniform(keys[4], (N_GX, N_GY, 6, CONTACTS_DEV), jnp.float32) ** level_of(keys[4], (N_GX, N_GY, 6, CONTACTS_DEV), ((0, 64), (1, 4)), -0.2, 0.2)), 0.1, 2.0)
    first_body = touch_ends(jax.random.randint(keys[5], (N_GX, N_GY, CONTACTS_DEV), 0, BODY_DEV), jax.random.fold_in(keys[5], 1), 0, BODY_DEV - 1).astype(jnp.int32)
    second_body = touch_ends(jax.random.randint(keys[6], (N_GX, N_GY, CONTACTS_DEV), 0, BODY_DEV + 8 * SEND), jax.random.fold_in(keys[6], 1), 0, (BODY_DEV + 8 * SEND) - 1).astype(jnp.int32)
    border_bodies = touch_ends(jax.random.randint(keys[7], (N_GX, N_GY, 8, SEND), 0, BODY_DEV), jax.random.fold_in(keys[7], 1), 0, BODY_DEV - 1).astype(jnp.int32)
    return {"body_load": body_load, "proximal": proximal, "contact_blocks": contact_blocks, "slacks": slacks, "dual_rows": dual_rows, "first_body": first_body, "second_body": second_body, "border_bodies": border_bodies}


DIRECTIONS = ((-1, -1), (-1, 0), (-1, 1), (0, -1), (0, 1), (1, -1), (1, 0), (1, 1))
HIGHEST = lax.Precision.HIGHEST

def per_tile(function):
    return jax.vmap(jax.vmap(function))

def deliver(buffers):
    count_x = buffers.shape[0]
    count_y = buffers.shape[1]
    padded = jnp.pad(buffers, ((1, 1), (1, 1), (0, 0), (0, 0), (0, 0)))
    pieces = []
    for slot_index, (shift_x, shift_y) in enumerate(DIRECTIONS):
        pieces.append(padded[1 + shift_x:1 + shift_x + count_x, 1 + shift_y:1 + shift_y + count_y, :, 7 - slot_index])
    return jnp.stack(pieces, axis=3)

def spread_ends(values, first_index, second_index, bodies, halo_slots):
    half_width = values.shape[0] // 2
    local_sums = jnp.zeros((half_width, bodies), jnp.float32).at[:, first_index].add(values[:half_width])
    extended = jnp.zeros((half_width, bodies + halo_slots), jnp.float32).at[:, second_index].add(values[half_width:])
    return (local_sums + extended[:, :bodies], extended[:, bodies:])

def take_border(body_field, border):
    return jnp.take(body_field, border.reshape(-1), axis=1).reshape(body_field.shape[0], 8, -1)

def add_border(body_field, returned, border):
    return body_field.at[:, border.reshape(-1)].add(returned.reshape(body_field.shape[0], -1))

def cholesky_six(matrix):
    entries = {}
    for column in range(6):
        partial_sum = matrix[column, column]
        for inner_index in range(column):
            partial_sum = partial_sum - entries[column, inner_index] * entries[column, inner_index]
        pivot_value = jnp.sqrt(partial_sum)
        entries[column, column] = pivot_value
        for row_index in range(column + 1, 6):
            row_sum = matrix[row_index, column]
            for inner_index in range(column):
                row_sum = row_sum - entries[row_index, inner_index] * entries[column, inner_index]
            entries[row_index, column] = row_sum / pivot_value
    zero_row = jnp.zeros_like(matrix[0, 0])
    return jnp.stack([jnp.stack([entries.get((row_index, column), zero_row) for column in range(6)]) for row_index in range(6)])

def block_solve(factor, rows_in):
    forward = []
    for row_index in range(6):
        partial_sum = rows_in[row_index]
        for inner_index in range(row_index):
            partial_sum = partial_sum - factor[row_index, inner_index] * forward[inner_index]
        forward.append(partial_sum / factor[row_index, row_index])
    backward = [None] * 6
    for row_index in reversed(range(6)):
        partial_sum = forward[row_index]
        for inner_index in range(row_index + 1, 6):
            partial_sum = partial_sum - factor[inner_index, row_index] * backward[inner_index]
        backward[row_index] = partial_sum / factor[row_index, row_index]
    return jnp.stack(backward)

def reference(body_load, proximal, contact_blocks, slacks, dual_rows, first_body, second_body, border_bodies):
    scaling = dual_rows / slacks
    bodies = body_load.shape[3]
    halo_slots = 8 * border_bodies.shape[3]

    def diagonal_terms(blocks, scale_rows, first_index, second_index):
        upper_blocks = jnp.einsum('rac,rc,rbc->abc', blocks[:, :6], scale_rows, blocks[:, :6], precision=HIGHEST).reshape(36, -1)
        lower_blocks = jnp.einsum('rac,rc,rbc->abc', blocks[:, 6:], scale_rows, blocks[:, 6:], precision=HIGHEST).reshape(36, -1)
        return spread_ends(jnp.concatenate([upper_blocks, lower_blocks], axis=0), first_index, second_index, bodies, halo_slots)
    diag_local, diag_back = per_tile(diagonal_terms)(contact_blocks, scaling, first_body, second_body)
    returned = deliver(diag_back.reshape(diag_back.shape[:3] + (8, -1)))
    diagonal = per_tile(add_border)(diag_local, returned, border_bodies)
    diagonal = diagonal.reshape(diagonal.shape[:2] + (6, 6, bodies))
    diagonal = diagonal + proximal[:, :, :, None, :] * jnp.eye(6, dtype=jnp.float32)[:, :, None]
    factor = per_tile(cholesky_six)(diagonal)

    def contact_image(body_field, halo_rows, blocks, scale_rows, first_index, second_index):
        extended = jnp.concatenate([body_field, halo_rows.reshape(6, -1)], axis=1)
        stacked = jnp.concatenate([jnp.take(body_field, first_index, axis=1), jnp.take(extended, second_index, axis=1)], axis=0)
        strain = jnp.einsum('rjc,jc->rc', blocks, stacked, precision=HIGHEST)
        values = jnp.einsum('rjc,rc->jc', blocks, scale_rows * strain, precision=HIGHEST)
        return spread_ends(values, first_index, second_index, bodies, halo_slots)

    def operate(direction):
        halo_rows = deliver(per_tile(take_border)(direction, border_bodies))
        image_local, image_back = per_tile(contact_image)(direction, halo_rows, contact_blocks, scaling, first_body, second_body)
        back_rows = deliver(image_back.reshape(image_back.shape[:3] + (8, -1)))
        return per_tile(add_border)(image_local, back_rows, border_bodies) + proximal * direction
    solution = jnp.zeros_like(body_load)
    residual = body_load
    preconditioned = per_tile(block_solve)(factor, residual)
    direction = preconditioned
    norm_now = jnp.sum(residual * preconditioned)
    for iteration in range(ITERS):
        image_field = operate(direction)
        step_length = norm_now / jnp.sum(direction * image_field)
        solution = solution + step_length * direction
        residual = residual - step_length * image_field
        preconditioned = per_tile(block_solve)(factor, residual)
        norm_next = jnp.sum(residual * preconditioned)
        direction = preconditioned + norm_next / norm_now * direction
        norm_now = norm_next
    return (solution, residual)
```

```python
import functools

import jax
import jax.numpy as jnp
from jax import lax
from jax.experimental import pallas as pl
from jax.experimental.pallas import tpu as pltpu
from jax.sharding import PartitionSpec as P

ITERS = 4
LANES = 128
ROWS = 8
SPAN = 256
GROUP = 512
SPLITS = 3
MESH = pl.DeviceIdType.MESH
OFFSETS = ((-1, -1), (-1, 0), (-1, 1), (0, -1), (0, 1), (1, -1), (1, 0), (1, 1))


def gather_columns(chunks, lane, chunk_of):
    picked = jnp.take_along_axis(chunks[0], lane, axis=1, mode="promise_in_bounds")
    for number in range(1, len(chunks)):
        other = jnp.take_along_axis(chunks[number], lane, axis=1, mode="promise_in_bounds")
        picked = jnp.where(chunk_of == number, other, picked)
    return picked


def split_terms(values):
    terms = []
    for number in range(SPLITS):
        term = values.astype(jnp.bfloat16).astype(jnp.float32)
        terms.append(term)
        if number + 1 < SPLITS:
            values = values - term
    return terms


def one_hot_dot(left, hot):
    return lax.dot_general(
        left, hot, (((1,), (1,)), ((), ())), preferred_element_type=jnp.float32
    )


def sum_rows(values):
    for shift in (4, 2, 1):
        values = values + pltpu.roll(values, shift, 0)
    return values


def wide(ref_value, lanes):
    return jnp.broadcast_to(ref_value, (ROWS, lanes))


def inverse_six(entry, width):
    lower, pivots = {}, []
    for column in range(6):
        scaled = [lower[column, inner] * pivots[inner][0] for inner in range(column)]
        value = entry(column, column)
        for inner in range(column):
            value = value - scaled[inner] * lower[column, inner]
        flipped = 1.0 / value
        pivots.append((value, flipped))
        for row in range(column + 1, 6):
            value = entry(row, column)
            for inner in range(column):
                value = value - lower[row, inner] * scaled[inner]
            lower[row, column] = value * flipped
    unit = {}
    for column in range(6):
        for row in range(column + 1, 6):
            value = -lower[row, column]
            for inner in range(column + 1, row):
                value = value - lower[row, inner] * unit[inner, column]
            unit[row, column] = value
    result = {}
    for row in range(6):
        for column in range(row + 1):
            value = None
            for inner in range(row, 6):
                left = pivots[inner][1]
                if inner > row:
                    left = left * unit[inner, row]
                if inner > column:
                    left = left * unit[inner, column]
                value = left if value is None else value + left
            result[row, column] = result[column, row] = value
    return result


def coefficients(moments):
    def inner(left, right):
        total = None
        for i, a in enumerate(left):
            for j, b in enumerate(right):
                term = a * b * moments[i + j]
                total = term if total is None else total + term
        return total

    one = jnp.ones_like(moments[0])
    step = [None] * ITERS
    residual, direction = [one], [one]
    norm_now = moments[0]
    for iteration in range(ITERS):
        image = []
        for j in range(len(direction) + 1):
            parts = [direction[i] for i in (j - 1, j) if 0 <= i < len(direction)]
            image.append(sum(parts[1:], parts[0]))
        length = norm_now / inner(direction, image)
        for j, value in enumerate(direction):
            step[j] = length * value if step[j] is None else step[j] + length * value
        residual = [
            (residual[j] - length * image[j]) if j < len(residual) else -length * image[j]
            for j in range(len(image))
        ]
        if iteration + 1 < ITERS:
            norm_next = inner(residual, residual)
            ratio = norm_next / norm_now
            direction = [
                (residual[j] + ratio * direction[j]) if j < len(direction) else residual[j]
                for j in range(len(residual))
            ]
            norm_now = norm_next
    return step, residual


def kernel(
    sizes,
    load_ref, prox_ref, block_ref, slack_ref, dual_ref, first_ref, second_ref, border_ref,
    step_ref, residual_ref,
    g1, g2, hot1, hot2, hotb, lane1, lane2, chunk1, chunk2, laneb, chunkb,
    left1, left2, leftb, basis_v, basis_q, prox8, inverse, diag, border_pad,
    diag_send, diag_recv, fore_send, fore_recv, back_send, back_recv,
    moment, part_recv, whole_send, whole_recv,
    diag_ssem, diag_rsem, fore_ssem, fore_rsem, back_ssem, back_rsem,
    part_ssem, part_rsem, whole_ssem, whole_rsem,
):
    nx, ny, ys, zs = sizes
    bodies, contacts = load_ref.shape[1], block_ref.shape[2]
    spans = bodies // SPAN
    chunks = bodies // LANES
    gx, gy = lax.axis_index("gx"), lax.axis_index("gy")
    z_at, y_at, core = gx // (2 * ys), (gx // 2) % ys, gx % 2

    near = [((gx + dx + nx) % nx, (gy + dy + ny) % ny) for dx, dy in OFFSETS]
    real = []
    for dx, dy in OFFSETS:
        to_x, to_y = gx + dx, gy + dy
        real.append((to_x >= 0) & (to_x < nx) & (to_y >= 0) & (to_y < ny))
    part_count, whole_count = ny * ys, zs * 2
    part_near, whole_near = [], []
    for offset in range(1, part_count):
        other = (gy * ys + y_at + offset) % part_count
        part_near.append((z_at * 2 * ys + (other % ys) * 2 + core, other // ys))
    for offset in range(1, whole_count):
        other = (z_at * 2 + core + offset) % whole_count
        whole_near.append(((other // 2) * 2 * ys + y_at * 2 + other % 2, gy))

    barrier = pltpu.get_barrier_semaphore()
    everyone = near + part_near + whole_near
    for device in everyone:
        pl.semaphore_signal(barrier, inc=1, device_id=device, device_id_type=MESH)

    first = wide(first_ref[...], contacts)
    second = wide(second_ref[...], contacts)
    lane1[...] = first % LANES
    chunk1[...] = first // LANES
    lane2[...] = second % LANES
    chunk2[...] = second // LANES
    border_pad[...] = jnp.zeros_like(border_pad)
    border_pad[:, : border_ref.shape[1]] = border_ref[...]
    lane_group = lax.broadcasted_iota(jnp.int32, (1, LANES), 1) // 32
    row_at = [border_pad[7 - place : 8 - place, :] for place in range(8)]
    border_rows = []
    for half in range(2):
        row = row_at[4 * half]
        for quarter in range(1, 4):
            row = jnp.where(
                lane_group == quarter,
                pltpu.roll(row_at[4 * half + quarter], 32 * quarter, 1),
                row,
            )
        border_rows.append(row)
    border = wide(jnp.concatenate(border_rows, axis=1), 2 * LANES)
    laneb[...] = border % LANES
    chunkb[...] = border // LANES

    for hot, index, count in ((hot1, first_ref[...], contacts), (hot2, second_ref[...], contacts)):
        for at in range(0, count, GROUP):
            spot = index[:, at : at + GROUP] % SPAN
            rows = lax.broadcasted_iota(jnp.int32, (SPAN, GROUP), 0)
            hot[:, at : at + GROUP] = jnp.where(rows == spot, 1.0, 0.0).astype(jnp.bfloat16)
    rows = lax.broadcasted_iota(jnp.int32, (SPAN, 2 * LANES), 0)
    hotb[...] = jnp.where(rows == border[0:1] % SPAN, 1.0, 0.0).astype(jnp.bfloat16)

    root = jnp.sqrt(dual_ref[...] / slack_ref[...])
    for r in range(6):
        head = block_ref[r, 0:8, :] * root[r : r + 1]
        tail = block_ref[r, 8:12, :] * root[r : r + 1]
        g1[r] = jnp.concatenate([head[0:6], head[0:2]], axis=0)
        g2[r] = jnp.concatenate([head[6:8], tail, head[6:8]], axis=0)
    zero_rows = jnp.zeros((2, bodies), jnp.float32)
    prox8[...] = jnp.concatenate([prox_ref[...], zero_rows], axis=0)
    basis_q[0] = jnp.concatenate([load_ref[...], zero_rows], axis=0)

    def put_first(target, at, base, values, span_of, width):
        for term in split_terms(values):
            masked = [jnp.where(span_of == s, term, 0.0) for s in range(spans)]
            target[base : base + ROWS * spans, at : at + width] = jnp.concatenate(
                masked, axis=0
            ).astype(jnp.bfloat16)
            base += ROWS * spans
        return base

    def put_second(target, at, base, values, span_of, width):
        base = put_first(target, at, base, values, span_of, width)
        terms = [jnp.where(span_of == spans, t, 0.0) for t in split_terms(values)]
        if len(terms) % 2:
            terms.append(jnp.zeros_like(terms[0]))
        target[base : base + ROWS * len(terms), at : at + width] = jnp.concatenate(
            terms, axis=0
        ).astype(jnp.bfloat16)
        return base + ROWS * len(terms)

    local_rows = ROWS * spans * SPLITS

    def local_sum(product, base):
        columns = []
        for s in range(spans):
            total = product[base + ROWS * s : base + ROWS * (s + 1)]
            for number in range(1, SPLITS):
                start = base + ROWS * (number * spans + s)
                total = total + product[start : start + ROWS]
            columns.append(total)
        return jnp.concatenate(columns, axis=1)

    def halo_sum(product, base):
        total = product[base : base + ROWS]
        for number in range(1, SPLITS):
            total = total + product[base + ROWS * number : base + ROWS * (number + 1)]
        return total

    def arrange(slots, place_of):
        halves = [None, None]
        for k in range(8):
            place = place_of(k)
            code = jnp.where(real[k], place % 4, -1)
            piece = jnp.where(lane_group == code, slots(k), 0.0)
            half = place // 4
            halves[half] = piece if halves[half] is None else halves[half] + piece
        return jnp.concatenate(halves, axis=1)

    def exchange(send, recv, ssem, rsem, place_of):
        copies = []
        for k, device in enumerate(near):
            copies.append(
                pltpu.make_async_remote_copy(
                    src_ref=send.at[place_of(k) // 4],
                    dst_ref=recv.at[7 - k],
                    send_sem=ssem.at[k],
                    recv_sem=rsem.at[7 - k],
                    device_id=device,
                    device_id_type=MESH,
                )
            )
            copies[-1].start()
        return copies

    def settle(copies):
        for copy in copies:
            copy.wait_send()
        for copy in copies:
            copy.wait_recv()

    reverse = lambda k: 7 - k
    forward = lambda k: k

    sub = lax.broadcasted_iota(jnp.int32, (ROWS, GROUP), 0)
    per_first, per_second = local_rows, left2.shape[0] // 3
    for at in range(0, contacts, GROUP):
        cols = slice(at, at + GROUP)
        for source, target, chunk_ref, put, per in (
            (g1, left1, chunk1, put_first, per_first),
            (g2, left2, chunk2, put_second, per_second),
        ):
            sums = [None] * 4
            for r in range(6):
                value = source[r, :, cols]
                for d in range(4):
                    term = value * (pltpu.roll(value, ROWS - d, 0) if d else value)
                    sums[d] = term if sums[d] is None else sums[d] + term
            span_of = chunk_ref[:, cols] // 2
            for d in range(3):
                packed = jnp.where(sub == 6, pltpu.roll(sums[3], 6 - d, 0), sums[d])
                put(target, at, d * per, packed, span_of, GROUP)
    product2 = one_hot_dot(left2[...], hot2[...])
    for d in range(3):
        halo = halo_sum(product2, d * per_second + local_rows)
        diag_send[0, d * ROWS : (d + 1) * ROWS, :] = halo[:, :LANES]
        diag_send[1, d * ROWS : (d + 1) * ROWS, :] = halo[:, LANES:]
    pl.semaphore_wait(barrier, len(everyone))
    copies = exchange(diag_send, diag_recv, diag_ssem, diag_rsem, forward)
    product1 = one_hot_dot(left1[...], hot1[...])
    for d in range(3):
        diag[d * ROWS : (d + 1) * ROWS, :] = local_sum(product1, d * per_first) + local_sum(
            product2, d * per_second
        )
    settle(copies)
    span_b = chunkb[...] // 2
    for d in range(3):
        returned = arrange(lambda k: diag_recv[k, d * ROWS : (d + 1) * ROWS, :], reverse)
        put_first(leftb, 0, d * per_first, returned, span_b, 2 * LANES)
    product = one_hot_dot(leftb[...], hotb[...])
    for d in range(3):
        rows = slice(d * ROWS, (d + 1) * ROWS)
        total = diag[rows, :] + local_sum(product, d * per_first)
        diag[rows, :] = total + prox8[...] if d == 0 else total

    def entry(row, column):
        d = (column - row) % 6
        if d == 3:
            at = min(row, column) * ROWS + 6
        elif d < 3:
            at = d * ROWS + row
        else:
            at = (6 - d) * ROWS + column
        return diag[at : at + 1, :]

    inverse[...] = jnp.zeros_like(inverse)
    for (row, column), value in inverse_six(entry, bodies).items():
        inverse[column, row : row + 1, :] = value

    def precondition(field):
        total = None
        for b in range(6):
            term = inverse[b] * wide(field[b : b + 1, :], bodies)
            total = term if total is None else total + term
        return total

    def dot_rows(left, right):
        product = left * right
        total = product[:, 0:LANES]
        for at in range(LANES, bodies, LANES):
            total = total + product[:, at : at + LANES]
        return total

    def cut(field, count):
        return [field[:, i * LANES : (i + 1) * LANES] for i in range(count)]

    basis_v[0] = precondition(basis_q[0])
    pending = []
    for k in range(ITERS):
        v_now, q_now = basis_v[k], basis_q[k]
        parts = cut(v_now, chunks)
        for half in range(2):
            cols = slice(half * LANES, (half + 1) * LANES)
            fore_send[k, half] = gather_columns(parts, laneb[:, cols], chunkb[:, cols])
        copies = exchange(fore_send.at[k], fore_recv.at[k], fore_ssem.at[k], fore_rsem.at[k], reverse)
        moment[2 * k : 2 * k + 1, :] = sum_rows(dot_rows(v_now, q_now))[0:1]
        settle(copies)
        extended = parts + cut(arrange(lambda s: fore_recv[k, s], forward), 2)
        energy = None
        for at in range(0, contacts, GROUP):
            cols = slice(at, at + GROUP)
            near_parts, far_parts = [], []
            for c in range(at, at + GROUP, LANES):
                spot = slice(c, c + LANES)
                near_parts.append(gather_columns(parts, lane1[:, spot], chunk1[:, spot]))
                far_parts.append(gather_columns(extended, lane2[:, spot], chunk2[:, spot]))
            u1 = jnp.concatenate(near_parts, axis=1)
            u2 = jnp.concatenate(far_parts, axis=1)
            w1 = w2 = None
            for r in range(6):
                a, b = g1[r, :, cols], g2[r, :, cols]
                strain = sum_rows(a * u1 + b * u2)
                w1 = a * strain if w1 is None else w1 + a * strain
                w2 = b * strain if w2 is None else w2 + b * strain
                if k == ITERS - 1:
                    energy = strain * strain if energy is None else energy + strain * strain
            put_first(left1, at, 0, w1, chunk1[:, cols] // 2, GROUP)
            put_second(left2, at, 0, w2, chunk2[:, cols] // 2, GROUP)
        if k == ITERS - 1:
            folded = energy[:, 0:LANES]
            for at in range(LANES, GROUP, LANES):
                folded = folded + energy[:, at : at + LANES]
            spring = sum_rows(dot_rows(v_now * prox8[...], v_now))
            moment[2 * k + 1 : 2 * k + 2, :] = (folded + spring)[0:1] - moment[2 * k : 2 * k + 1, :]
            part_copies = []
            for number, device in enumerate(part_near):
                part_copies.append(
                    pltpu.make_async_remote_copy(
                        src_ref=moment,
                        dst_ref=part_recv.at[number],
                        send_sem=part_ssem.at[number],
                        recv_sem=part_rsem.at[number],
                        device_id=device,
                        device_id_type=MESH,
                    )
                )
                part_copies[-1].start()
        product2 = one_hot_dot(left2[0:per_second], hot2[...])
        halo = halo_sum(product2, local_rows)
        back_send[k, 0] = halo[:, :LANES]
        back_send[k, 1] = halo[:, LANES:]
        copies = exchange(back_send.at[k], back_recv.at[k], back_ssem.at[k], back_rsem.at[k], forward)
        if k == ITERS - 1:
            settle(part_copies)
            total = moment[...]
            for number in range(len(part_near)):
                total = total + part_recv[number]
            whole_send[...] = total
            whole_copies = []
            for number, device in enumerate(whole_near):
                whole_copies.append(
                    pltpu.make_async_remote_copy(
                        src_ref=whole_send,
                        dst_ref=whole_recv.at[number],
                        send_sem=whole_ssem.at[number],
                        recv_sem=whole_rsem.at[number],
                        device_id=device,
                        device_id_type=MESH,
                    )
                )
                whole_copies[-1].start()
        product1 = one_hot_dot(left1[0:per_first], hot1[...])
        image = local_sum(product1, 0) + local_sum(product2, 0) + prox8[...] * v_now - q_now
        settle(copies)
        returned = arrange(lambda s: back_recv[k, s], reverse)
        put_first(leftb, 0, 0, returned, span_b, 2 * LANES)
        q_next = image + local_sum(one_hot_dot(leftb[0:per_first], hotb[...]), 0)
        basis_q[k + 1] = q_next
        if k < ITERS - 1:
            moment[2 * k + 1 : 2 * k + 2, :] = sum_rows(dot_rows(v_now, q_next))[0:1]
            basis_v[k + 1] = precondition(q_next)

    settle(whole_copies)
    total = whole_send[...]
    for number in range(len(whole_near)):
        total = total + whole_recv[number]
    sums = jnp.sum(total, axis=1, keepdims=True)
    moments = [jnp.broadcast_to(sums[i : i + 1, :], (ROWS, LANES)) for i in range(2 * ITERS)]
    along, left = coefficients(moments)
    for c in range(chunks):
        cols = slice(c * LANES, (c + 1) * LANES)
        value = along[0] * basis_v[0, :, cols]
        for j in range(1, ITERS):
            value = value + along[j] * basis_v[j, :, cols]
        step_ref[:, cols] = value[0:6]
        value = left[0] * basis_q[0, :, cols]
        for j in range(1, ITERS + 1):
            value = value + left[j] * basis_q[j, :, cols]
        residual_ref[:, cols] = value[0:6]


def local(mesh_shape, body_load, proximal, contact_blocks, slacks, dual_rows, first_body, second_body, border_bodies):
    nx, ny = mesh_shape
    ys = 4 if nx % 8 == 0 else 1
    zs = nx // (2 * ys)
    bodies, contacts = body_load.shape[3], contact_blocks.shape[4]
    spans = bodies // SPAN
    halves = SPLITS + SPLITS % 2
    first_rows, second_rows = ROWS * spans * SPLITS, ROWS * (spans * SPLITS + halves)
    f32, bf16, i32 = jnp.float32, jnp.bfloat16, jnp.int32
    vmem = pltpu.VMEM
    dma = pltpu.SemaphoreType.DMA
    parts, wholes = ny * ys - 1, 2 * zs - 1
    scratch = [
        vmem((6, ROWS, contacts), f32),
        vmem((6, ROWS, contacts), f32),
        vmem((SPAN, contacts), bf16),
        vmem((SPAN, contacts), bf16),
        vmem((SPAN, 2 * LANES), bf16),
        vmem((ROWS, contacts), i32),
        vmem((ROWS, contacts), i32),
        vmem((ROWS, contacts), i32),
        vmem((ROWS, contacts), i32),
        vmem((ROWS, 2 * LANES), i32),
        vmem((ROWS, 2 * LANES), i32),
        vmem((3 * first_rows, contacts), bf16),
        vmem((3 * second_rows, contacts), bf16),
        vmem((3 * first_rows, 2 * LANES), bf16),
        vmem((ITERS, ROWS, bodies), f32),
        vmem((ITERS + 1, ROWS, bodies), f32),
        vmem((ROWS, bodies), f32),
        vmem((6, ROWS, bodies), f32),
        vmem((3 * ROWS, bodies), f32),
        vmem((ROWS, LANES), i32),
        vmem((2, 3 * ROWS, LANES), f32),
        vmem((8, 3 * ROWS, LANES), f32),
        vmem((ITERS, 2, ROWS, LANES), f32),
        vmem((ITERS, 8, ROWS, LANES), f32),
        vmem((ITERS, 2, ROWS, LANES), f32),
        vmem((ITERS, 8, ROWS, LANES), f32),
        vmem((ROWS, LANES), f32),
        vmem((parts, ROWS, LANES), f32),
        vmem((ROWS, LANES), f32),
        vmem((wholes, ROWS, LANES), f32),
        dma((8,)),
        dma((8,)),
        dma((ITERS, 8)),
        dma((ITERS, 8)),
        dma((ITERS, 8)),
        dma((ITERS, 8)),
        dma((parts,)),
        dma((parts,)),
        dma((wholes,)),
        dma((wholes,)),
    ]
    step, residual = pl.pallas_call(
        functools.partial(kernel, (nx, ny, ys, zs)),
        out_shape=[jax.ShapeDtypeStruct((6, bodies), f32)] * 2,
        in_specs=[pl.BlockSpec(memory_space=pltpu.VMEM)] * 8,
        out_specs=[pl.BlockSpec(memory_space=pltpu.VMEM)] * 2,
        scratch_shapes=scratch,
        compiler_params=pltpu.CompilerParams(
            collective_id=0, has_side_effects=True, vmem_limit_bytes=48 * 1024 * 1024
        ),
    )(
        body_load[0, 0],
        proximal[0, 0],
        contact_blocks[0, 0],
        slacks[0, 0],
        dual_rows[0, 0],
        first_body[0],
        second_body[0],
        border_bodies[0, 0],
    )
    return step[None, None], residual[None, None]


def solution(mesh):
    return jax.shard_map(
        functools.partial(local, (mesh.shape["gx"], mesh.shape["gy"])),
        mesh=mesh,
        in_specs=(
            P("gx", "gy", None, None),
            P("gx", "gy", None, None),
            P("gx", "gy", None, None, None),
            P("gx", "gy", None, None),
            P("gx", "gy", None, None),
            P("gx", "gy", None),
            P("gx", "gy", None),
            P("gx", "gy", None, None),
        ),
        out_specs=(P("gx", "gy", None, None), P("gx", "gy", None, None)),
        check_vma=False,
    )
```

```python
import functools

import jax
import jax.numpy as jnp
from jax import lax
from jax.experimental import pallas as pl
from jax.experimental.pallas import tpu as pltpu
from jax.sharding import PartitionSpec as P

ITERS = 4
LANES = 128
ROWS = 8
SPAN = 256
SPLITS = 3
FIELDS = 6
PAIRS = [(a, b) for a in range(FIELDS) for b in range(a, FIELDS)]
PAIR_ROWS = 24
MESH = pl.DeviceIdType.MESH
OFFSETS = ((-1, -1), (-1, 0), (-1, 1), (0, -1), (0, 1), (1, -1), (1, 0), (1, 1))
SEND_ORDER = (0, 2, 5, 7, 1, 6, 3, 4)


def pick(source, lane):
    return jnp.take_along_axis(source, lane, axis=1, mode="promise_in_bounds")


def add_up(values):
    total = values[0]
    for value in values[1:]:
        total = total + value
    return total


def split_terms(values):
    terms = []
    for number in range(SPLITS):
        term = values.astype(jnp.bfloat16).astype(jnp.float32)
        terms.append(term)
        if number + 1 < SPLITS:
            values = values - term
    return terms


def dot(left, hot):
    return lax.dot_general(
        left, hot, (((1,), (0,)), ((), ())), preferred_element_type=jnp.float32
    )


def sum_rows(values):
    for shift in (4, 2, 1):
        values = values + pltpu.roll(values, shift, 0)
    return values


def inverse_six(entry):
    lower, flipped = {}, []
    for column in range(6):
        scaled = [lower[column, inner] * flipped[inner][0] for inner in range(column)]
        value = entry(column, column)
        for inner in range(column):
            value = value - scaled[inner] * lower[column, inner]
        flipped.append((value, 1.0 / value))
        for row in range(column + 1, 6):
            value = entry(column, row)
            for inner in range(column):
                value = value - lower[row, inner] * scaled[inner]
            lower[row, column] = value * flipped[column][1]
    unit = {}
    for column in range(6):
        for row in range(column + 1, 6):
            value = -lower[row, column]
            for inner in range(column + 1, row):
                value = value - lower[row, inner] * unit[inner, column]
            unit[row, column] = value
    result = {}
    for row in range(6):
        weighted = {inner: flipped[inner][1] * unit[inner, row] for inner in range(row + 1, 6)}
        weighted[row] = flipped[row][1]
        for column in range(row + 1):
            terms = []
            for inner in range(row, 6):
                term = weighted[inner]
                terms.append(term if inner == column else term * unit[inner, column])
            result[row, column] = result[column, row] = add_up(terms)
    return result


def coefficients(moments):
    def inner(left, right):
        weights = {}
        for i, a in enumerate(left):
            for j, b in enumerate(right):
                weights.setdefault(i + j, []).append(a * b)
        return add_up([add_up(w) * moments[i] for i, w in weights.items()])

    one = jnp.ones_like(moments[0])
    step = [None] * ITERS
    residual, direction = [one], [one]
    norm_now = moments[0]
    for iteration in range(ITERS):
        image = []
        for j in range(len(direction) + 1):
            image.append(add_up([direction[i] for i in (j - 1, j) if 0 <= i < len(direction)]))
        length = norm_now / inner(direction, image)
        for j, value in enumerate(direction):
            step[j] = length * value if step[j] is None else step[j] + length * value
        residual = [
            (residual[j] - length * image[j]) if j < len(residual) else -length * image[j]
            for j in range(len(image))
        ]
        if iteration + 1 < ITERS:
            norm_next = inner(residual, residual)
            ratio = norm_next / norm_now
            direction = [
                (residual[j] + ratio * direction[j]) if j < len(direction) else residual[j]
                for j in range(len(residual))
            ]
            norm_now = norm_next
    return step, residual


def kernel(
    sizes,
    load_hbm, prox_hbm, block_hbm, slack_hbm, dual_hbm, first_hbm, second_hbm, border_hbm,
    step_ref, residual_ref,
    load_in, prox_in, block_in, slack_in, dual_in, first_in, second_in, border_in, in_sem,
    g, hot1, hot2, hotb, span1, span2, spanb, laneb, chunkb, border_pad,
    left1, left2, left_halo, leftb, spread, spread_first, spread_pairs, spread_pairs_first,
    basis_v, basis_q, prox, inverse, diag, returned, columns,
    diag_send, diag_recv, fore_send, fore_recv, back_send, back_recv,
    part_send, part_recv, whole_send, whole_recv,
    diag_ssem, diag_rsem, fore_ssem, fore_rsem, back_ssem, back_rsem,
    part_ssem, part_rsem, whole_ssem, whole_rsem,
):
    nx, ny, ys, zs = sizes
    chunks = load_in.shape[0] // FIELDS
    spans = chunks * LANES // SPAN
    tiles = first_in.shape[0]
    f32, bf16 = jnp.float32, jnp.bfloat16
    gx, gy = lax.axis_index("gx"), lax.axis_index("gy")
    z_at, y_at, core = gx // (2 * ys), (gx // 2) % ys, gx % 2

    loads = []
    for number, (source, target) in enumerate(
        (
            (second_hbm, second_in),
            (block_hbm, block_in),
            (slack_hbm, slack_in),
            (dual_hbm, dual_in),
            (first_hbm, first_in),
            (border_hbm, border_in),
            (load_hbm, load_in),
            (prox_hbm, prox_in),
        )
    ):
        loads.append(pltpu.make_async_copy(source, target, in_sem.at[number]))
        loads[-1].start()

    near = [((gx + dx + nx) % nx, (gy + dy + ny) % ny) for dx, dy in OFFSETS]
    real = []
    for dx, dy in OFFSETS:
        to_x, to_y = gx + dx, gy + dy
        real.append((to_x >= 0) & (to_x < nx) & (to_y >= 0) & (to_y < ny))
    part_count, whole_count = ny * ys, zs * 2
    part_near, whole_near = [], []
    for offset in range(1, part_count):
        other = (gy * ys + y_at + offset) % part_count
        part_near.append((z_at * 2 * ys + (other % ys) * 2 + core, other // ys))
    for offset in range(1, whole_count):
        other = (z_at * 2 + core + offset) % whole_count
        whole_near.append(((other // 2) * 2 * ys + y_at * 2 + other % 2, gy))
    barrier = pltpu.get_barrier_semaphore()
    everyone = near + part_near + whole_near
    for device in everyone:
        pl.semaphore_signal(barrier, inc=1, device_id=device, device_id_type=MESH)

    lane_group = lax.broadcasted_iota(jnp.int32, (1, LANES), 1) // 32
    lane_at = lax.broadcasted_iota(jnp.int32, (LANES, LANES), 1)

    def build_hot(hot, row, at):
        spot = jnp.transpose(jnp.broadcast_to(row % SPAN, (LANES, LANES)).astype(f32))
        for part in range(SPAN // LANES):
            same = spot == (lane_at + part * LANES).astype(f32)
            hot[at : at + LANES, part * LANES : (part + 1) * LANES] = jnp.where(
                same, 1.0, 0.0
            ).astype(bf16)

    def write_terms(target, values, masks):
        pieces = [jnp.where(mask, t, 0.0) for t in split_terms(values) for mask in masks]
        if (len(pieces) * values.shape[1]) % 16:
            pieces.append(jnp.zeros((values.shape[0], ROWS, LANES), f32))
        packed = jnp.concatenate(pieces, axis=1).astype(bf16)
        for s in range(values.shape[0]):
            target[0 : packed.shape[1], s * LANES : (s + 1) * LANES] = packed[s]
        return packed.shape[1]

    def read_terms(product, rows, masks):
        result = []
        for mask in range(masks):
            total = add_up(
                [
                    product[(n * masks + mask) * rows : (n * masks + mask + 1) * rows]
                    for n in range(SPLITS)
                ]
            )
            result.extend([total[:, :LANES], total[:, LANES:]])
        return result

    def arrange(slots, place_of):
        halves = [[], []]
        for k in range(8):
            place = place_of(k)
            code = jnp.where(real[k], place % 4, -1)
            halves[place // 4].append(jnp.where(lane_group == code, slots(k), 0.0))
        return [add_up(half) for half in halves]

    def reverse(k):
        return 7 - k

    def forward(k):
        return k

    def exchange(send, recv, ssem, rsem, place_of):
        copies = []
        for k in SEND_ORDER:
            copies.append(
                pltpu.make_async_remote_copy(
                    src_ref=send.at[place_of(k) // 4],
                    dst_ref=recv.at[7 - k],
                    send_sem=ssem.at[k],
                    recv_sem=rsem.at[7 - k],
                    device_id=near[k],
                    device_id_type=MESH,
                )
            )
            copies[-1].start()
        return copies

    def broadcast_all(sender, receiver, ssem, rsem, devices):
        copies = []
        for number, device in enumerate(devices):
            copies.append(
                pltpu.make_async_remote_copy(
                    src_ref=sender,
                    dst_ref=receiver.at[number],
                    send_sem=ssem.at[number],
                    recv_sem=rsem.at[number],
                    device_id=device,
                    device_id_type=MESH,
                )
            )
            copies[-1].start()
        return copies

    def sent(copies):
        for copy in copies:
            copy.wait_send()

    def arrived(copies):
        for copy in copies:
            copy.wait_recv()

    spread[...] = jnp.zeros_like(spread)
    spread_first[...] = jnp.zeros_like(spread_first)
    spread_pairs[...] = jnp.zeros_like(spread_pairs)
    spread_pairs_first[...] = jnp.zeros_like(spread_pairs_first)
    loads[0].wait()
    for s in range(tiles):
        row = second_in[s : s + 1, :]
        span2[s] = jnp.broadcast_to(row // SPAN, (ROWS, LANES))
        build_hot(hot2, row, s * LANES)

    def masks_of(span, rows, wanted):
        value = span[...]
        if rows != ROWS:
            value = jnp.concatenate([value] * (rows // ROWS), axis=1)
        return [value == number for number in wanted]

    def pair_products(base, target):
        for p, (a, b) in enumerate(PAIRS):
            value = add_up([g[r * 12 + base + a] * g[r * 12 + base + b] for r in range(6)])
            target[pl.ds(p, tiles, stride=PAIR_ROWS), :] = value

    for number in (1, 2, 3):
        loads[number].wait()
    root = [jnp.sqrt(dual_in[r] / slack_in[r]) for r in range(6)]
    for r in range(6):
        for j in range(6, 12):
            g[r * 12 + j] = block_in[r * 12 + j] * root[r]
    pair_products(6, spread_pairs)
    pair_values = spread_pairs[...].reshape(tiles, PAIR_ROWS, LANES)
    rows = write_terms(left_halo, pair_values, masks_of(span2, PAIR_ROWS, [spans]))
    halves = read_terms(dot(left_halo[0:rows, :], hot2[...]), PAIR_ROWS, 1)
    for half in range(2):
        diag_send[half] = halves[half]
    pl.semaphore_wait(barrier, len(everyone))
    copies = exchange(diag_send, diag_recv, diag_ssem, diag_rsem, forward)

    rows = write_terms(left2, pair_values, masks_of(span2, PAIR_ROWS, range(spans)))
    local2 = read_terms(dot(left2[0:rows, :], hot2[...]), PAIR_ROWS, spans)
    for r in range(6):
        for j in range(6):
            g[r * 12 + j] = block_in[r * 12 + j] * root[r]
    pair_products(0, spread_pairs_first)
    loads[4].wait()
    for s in range(tiles):
        row = first_in[s : s + 1, :]
        span1[s] = jnp.broadcast_to(row // SPAN, (ROWS, LANES))
        build_hot(hot1, row, s * LANES)
    pair_values = spread_pairs_first[...].reshape(tiles, PAIR_ROWS, LANES)
    rows = write_terms(left1, pair_values, masks_of(span1, PAIR_ROWS, range(spans)))
    local1 = read_terms(dot(left1[0:rows, :], hot1[...]), PAIR_ROWS, spans)
    for c in range(chunks):
        diag[c] = local1[c] + local2[c]
    loads[5].wait()
    border_pad[...] = jnp.zeros_like(border_pad)
    border_pad[:, : border_in.shape[1]] = border_in[...]
    for half in range(2):
        row = border_pad[7 - 4 * half : 8 - 4 * half, :]
        for quarter in range(1, 4):
            place = 4 * half + quarter
            moved = pltpu.roll(border_pad[7 - place : 8 - place, :], 32 * quarter, 1)
            row = jnp.where(lane_group == quarter, moved, row)
        build_hot(hotb, row, half * LANES)
        whole = jnp.broadcast_to(row, (ROWS, LANES))
        laneb[half] = whole % LANES
        chunkb[half] = whole // LANES
        spanb[half] = whole // SPAN
    loads[6].wait()
    loads[7].wait()
    zero_rows = jnp.zeros((ROWS - FIELDS, LANES), f32)
    for c in range(chunks):
        basis_q[0, c] = jnp.concatenate(
            [load_in[pl.ds(c, FIELDS, stride=chunks), :], zero_rows], axis=0
        )
        prox[c] = jnp.concatenate(
            [prox_in[pl.ds(c, FIELDS, stride=chunks), :], zero_rows], axis=0
        )
    inverse[...] = jnp.zeros_like(inverse)
    columns[...] = jnp.zeros_like(columns)
    lane1, chunk1 = first_in[...] % LANES, first_in[...] // LANES
    lane2, chunk2 = second_in[...] % LANES, second_in[...] // LANES

    sent(copies)
    arrived(copies)
    halves = arrange(lambda k: diag_recv[k], reverse)
    for half in range(2):
        returned[half] = halves[half]
    rows = write_terms(leftb, returned[...], masks_of(spanb, PAIR_ROWS, range(spans)))
    localb = read_terms(dot(leftb[0:rows, :], hotb[...]), PAIR_ROWS, spans)
    entries = {}
    for c in range(chunks):
        spread_pairs[pl.ds(c, PAIR_ROWS, stride=ROWS), :] = diag[c] + localb[c]
    for p, (a, b) in enumerate(PAIRS):
        value = spread_pairs[p * ROWS : p * ROWS + chunks, :]
        if a == b:
            value = value + prox_in[a * chunks : (a + 1) * chunks, :]
        entries[a, b] = value
    for (a, b), value in inverse_six(lambda a, b: entries[a, b]).items():
        inverse[pl.ds(b * chunks * ROWS + a, chunks, stride=ROWS), :] = value

    def precondition(field):
        result = []
        for c in range(chunks):
            terms = []
            for b in range(FIELDS):
                at = (b * chunks + c) * ROWS
                terms.append(
                    inverse[at : at + ROWS, :]
                    * jnp.broadcast_to(field[c][b : b + 1, :], (ROWS, LANES))
                )
            result.append(add_up(terms))
        return result

    moments = jnp.zeros((1, LANES), f32)
    moment_group = lax.broadcasted_iota(jnp.int32, (1, LANES), 1) // 16

    def fold(value):
        value = sum_rows(value)[0:1]
        for shift in (64, 32, 16):
            value = value + pltpu.roll(value, shift, 1)
        return value

    def inner(left, right):
        return fold(add_up([left[c] * right[c] for c in range(chunks)]))

    def gather_fields(rows_of, lane, chunk, start, count):
        result = []
        for f in range(FIELDS):
            value = None
            for n in range(count):
                source = jnp.broadcast_to(rows_of(f, n), (tiles, LANES))
                piece = pick(source, lane)
                if value is None:
                    value = piece if start == 0 else jnp.where(chunk == start, piece, 0.0)
                else:
                    value = jnp.where(chunk == start + n, piece, value)
            result.append(value)
        return result

    q_now = [basis_q[0, c] for c in range(chunks)]
    v_now = precondition(q_now)
    late = []
    for k in range(ITERS):
        for c in range(chunks):
            basis_v[k, c] = v_now[c]
        ends = []
        for half in range(2):
            value = pick(v_now[0], laneb[half])
            for c in range(1, chunks):
                value = jnp.where(chunkb[half] == c, pick(v_now[c], laneb[half]), value)
            ends.append(value)
            fore_send[k, half] = value
        fore = exchange(
            fore_send.at[k], fore_recv.at[k], fore_ssem.at[k], fore_rsem.at[k], reverse
        )
        u1 = gather_fields(lambda f, n: basis_v[k, n, f : f + 1, :], lane1, chunk1, 0, chunks)
        u2 = gather_fields(lambda f, n: basis_v[k, n, f : f + 1, :], lane2, chunk2, 0, chunks)
        here = chunk2 < chunks
        u2 = [jnp.where(here, value, 0.0) for value in u2]
        strain = []
        for r in range(6):
            strain.append(
                add_up(
                    [g[r * 12 + j] * u1[j] for j in range(6)]
                    + [g[r * 12 + 6 + j] * u2[j] for j in range(6)]
                )
            )
        for j in range(6):
            value = add_up([g[r * 12 + 6 + j] * strain[r] for r in range(6)])
            spread[pl.ds(j, tiles, stride=ROWS), :] = value
        pulls = spread[...].reshape(tiles, ROWS, LANES)
        rows = write_terms(left_halo, pulls, masks_of(span2, ROWS, [spans]))
        halves = read_terms(dot(left_halo[0:rows, :], hot2[...]), ROWS, 1)
        for half in range(2):
            back_send[k, half] = halves[half]
        back = exchange(
            back_send.at[k], back_recv.at[k], back_ssem.at[k], back_rsem.at[k], forward
        )
        rows = write_terms(left2, pulls, masks_of(span2, ROWS, range(spans)))
        image = read_terms(dot(left2[0:rows, :], hot2[...]), ROWS, spans)
        image = [image[c] + prox[c] * v_now[c] - q_now[c] for c in range(chunks)]
        pushes = [add_up([g[r * 12 + j] * strain[r] for r in range(6)]) for j in range(6)]
        if k == 0:
            for p, (a, b) in enumerate(PAIRS):
                for half in range(2):
                    row = returned[half, p : p + 1, :]
                    columns[b, half, a : a + 1, :] = row
                    if a != b:
                        columns[a, half, b : b + 1, :] = row
        pulled = []
        for half in range(2):
            pulled.append(
                add_up(
                    [
                        columns[b, half]
                        * jnp.broadcast_to(ends[half][b : b + 1, :], (ROWS, LANES))
                        for b in range(FIELDS)
                    ]
                )
            )
        norm = inner(v_now, q_now)
        moments = jnp.where(moment_group == 2 * k, norm, moments)
        sent(late)
        sent(fore)
        arrived(fore)
        beyond = arrange(lambda s: fore_recv[k, s], forward)
        u2 = gather_fields(lambda f, n: beyond[n][f : f + 1, :], lane2, chunk2, chunks, 2)
        more = [
            add_up([g[r * 12 + 6 + j] * u2[j] for j in range(6)]) for r in range(6)
        ]
        for j in range(6):
            value = pushes[j] + add_up([g[r * 12 + j] * more[r] for r in range(6)])
            spread_first[pl.ds(j, tiles, stride=ROWS), :] = value
        if k == ITERS - 1:
            energy = add_up([(strain[r] + more[r]) * (strain[r] + more[r]) for r in range(6)])
            energy = add_up([energy[t : t + ROWS] for t in range(0, tiles, ROWS)])
            energy = energy + add_up([prox[c] * v_now[c] * v_now[c] for c in range(chunks)])
            last = fold(energy) - norm
            part_send[...] = jnp.where(moment_group == 2 * k + 1, last, moments)
            part = broadcast_all(part_send, part_recv, part_ssem, part_rsem, part_near)
        values = spread_first[...].reshape(tiles, ROWS, LANES)
        rows = write_terms(left1, values, masks_of(span1, ROWS, range(spans)))
        pushed = read_terms(dot(left1[0:rows, :], hot1[...]), ROWS, spans)
        image = [image[c] + pushed[c] for c in range(chunks)]
        arrived(back)
        late = back
        halves = arrange(lambda s: back_recv[k, s], reverse)
        values = jnp.concatenate([(halves[h] + pulled[h])[None] for h in range(2)], axis=0)
        rows = write_terms(leftb, values, masks_of(spanb, ROWS, range(spans)))
        added = read_terms(dot(leftb[0:rows, :], hotb[...]), ROWS, spans)
        q_next = [image[c] + added[c] for c in range(chunks)]
        for c in range(chunks):
            basis_q[k + 1, c] = q_next[c]
        if k < ITERS - 1:
            v_next = precondition(q_next)
            moments = jnp.where(moment_group == 2 * k + 1, inner(v_now, q_next), moments)
            q_now, v_now = q_next, v_next

    sent(late)
    sent(part)
    arrived(part)
    whole_send[...] = part_send[...] + add_up([part_recv[n] for n in range(len(part_near))])
    copies = broadcast_all(whole_send, whole_recv, whole_ssem, whole_rsem, whole_near)
    sent(copies)
    arrived(copies)
    total = whole_send[...] + add_up([whole_recv[n] for n in range(len(whole_near))])
    row_at = lax.broadcasted_iota(jnp.int32, (ROWS, LANES), 0)
    group_at = lax.broadcasted_iota(jnp.int32, (ROWS, LANES), 1) // 16
    total = jnp.where(row_at == group_at, jnp.broadcast_to(total, (ROWS, LANES)), 0.0)
    sums = jnp.sum(total, axis=1, keepdims=True)
    along, left = coefficients(
        [jnp.broadcast_to(sums[i : i + 1, :], (ROWS, LANES)) for i in range(2 * ITERS)]
    )
    for c in range(chunks):
        value = add_up([along[j] * basis_v[j, c] for j in range(ITERS)])
        step_ref[pl.ds(c, FIELDS, stride=chunks), :] = value[0:FIELDS]
        value = add_up([left[j] * basis_q[j, c] for j in range(ITERS + 1)])
        residual_ref[pl.ds(c, FIELDS, stride=chunks), :] = value[0:FIELDS]


def local(mesh_shape, body_load, proximal, contact_blocks, slacks, dual_rows, first_body, second_body, border_bodies):
    nx, ny = mesh_shape
    ys = 4 if nx % 8 == 0 else 1
    zs = nx // (2 * ys)
    bodies, contacts = body_load.shape[3], contact_blocks.shape[4]
    chunks, tiles, spans = bodies // LANES, contacts // LANES, bodies // SPAN
    f32, bf16, i32 = jnp.float32, jnp.bfloat16, jnp.int32
    vmem = pltpu.VMEM
    dma = pltpu.SemaphoreType.DMA
    parts, wholes = ny * ys - 1, 2 * zs - 1
    pair_rows = PAIR_ROWS * SPLITS
    operands = (
        body_load.reshape(FIELDS * chunks, LANES),
        proximal.reshape(FIELDS * chunks, LANES),
        contact_blocks.reshape(12 * FIELDS, tiles, LANES),
        slacks.reshape(FIELDS, tiles, LANES),
        dual_rows.reshape(FIELDS, tiles, LANES),
        first_body.reshape(tiles, LANES),
        second_body.reshape(tiles, LANES),
        border_bodies.reshape(border_bodies.shape[2:]),
    )
    scratch = [vmem(a.shape, a.dtype) for a in operands] + [
        dma((8,)),
        vmem((12 * FIELDS, tiles, LANES), f32),
        vmem((contacts, SPAN), bf16),
        vmem((contacts, SPAN), bf16),
        vmem((2 * LANES, SPAN), bf16),
        vmem((tiles, ROWS, LANES), i32),
        vmem((tiles, ROWS, LANES), i32),
        vmem((2, ROWS, LANES), i32),
        vmem((2, ROWS, LANES), i32),
        vmem((2, ROWS, LANES), i32),
        vmem((ROWS, LANES), i32),
        vmem((pair_rows * spans, contacts), bf16),
        vmem((pair_rows * spans, contacts), bf16),
        vmem((pair_rows + ROWS, contacts), bf16),
        vmem((pair_rows * spans, 2 * LANES), bf16),
        vmem((tiles * ROWS, LANES), f32),
        vmem((tiles * ROWS, LANES), f32),
        vmem((tiles * PAIR_ROWS, LANES), f32),
        vmem((tiles * PAIR_ROWS, LANES), f32),
        vmem((ITERS, chunks, ROWS, LANES), f32),
        vmem((ITERS + 1, chunks, ROWS, LANES), f32),
        vmem((chunks, ROWS, LANES), f32),
        vmem((FIELDS * chunks * ROWS, LANES), f32),
        vmem((chunks, PAIR_ROWS, LANES), f32),
        vmem((2, PAIR_ROWS, LANES), f32),
        vmem((FIELDS, 2, ROWS, LANES), f32),
        vmem((2, PAIR_ROWS, LANES), f32),
        vmem((8, PAIR_ROWS, LANES), f32),
        vmem((ITERS, 2, ROWS, LANES), f32),
        vmem((ITERS, 8, ROWS, LANES), f32),
        vmem((ITERS, 2, ROWS, LANES), f32),
        vmem((ITERS, 8, ROWS, LANES), f32),
        vmem((1, LANES), f32),
        vmem((parts, 1, LANES), f32),
        vmem((1, LANES), f32),
        vmem((wholes, 1, LANES), f32),
        dma((8,)),
        dma((8,)),
        dma((ITERS, 8)),
        dma((ITERS, 8)),
        dma((ITERS, 8)),
        dma((ITERS, 8)),
        dma((parts,)),
        dma((parts,)),
        dma((wholes,)),
        dma((wholes,)),
    ]
    step, residual = pl.pallas_call(
        functools.partial(kernel, (nx, ny, ys, zs)),
        out_shape=[jax.ShapeDtypeStruct((FIELDS * chunks, LANES), f32)] * 2,
        in_specs=[pl.BlockSpec(memory_space=pl.ANY)] * 8,
        out_specs=[pl.BlockSpec(memory_space=pltpu.VMEM)] * 2,
        scratch_shapes=scratch,
        compiler_params=pltpu.CompilerParams(
            collective_id=0, has_side_effects=True, vmem_limit_bytes=56 * 1024 * 1024
        ),
    )(*operands)
    return step.reshape(body_load.shape), residual.reshape(body_load.shape)


def solution(mesh):
    return jax.shard_map(
        functools.partial(local, (mesh.shape["gx"], mesh.shape["gy"])),
        mesh=mesh,
        in_specs=(
            P("gx", "gy", None, None),
            P("gx", "gy", None, None),
            P("gx", "gy", None, None, None),
            P("gx", "gy", None, None),
            P("gx", "gy", None, None),
            P("gx", "gy", None),
            P("gx", "gy", None),
            P("gx", "gy", None, None),
        ),
        out_specs=(P("gx", "gy", None, None), P("gx", "gy", None, None)),
        check_vma=False,
    )
```

```python
import functools

import jax
import jax.numpy as jnp
from jax import lax
from jax.experimental import pallas as pl
from jax.experimental.pallas import tpu as pltpu
from jax.sharding import PartitionSpec as P

ITERS = 4
LANES = 128
ROWS = 8
SPAN = 256
SPLITS = 3
FIELDS = 6
PAIRS = [(a, b) for a in range(FIELDS) for b in range(a, FIELDS)]
PAIR_ROWS = 24
MESH = pl.DeviceIdType.MESH
OFFSETS = ((-1, -1), (-1, 0), (-1, 1), (0, -1), (0, 1), (1, -1), (1, 0), (1, 1))
FAR = (0, 2, 5, 7)
CLOSE = (1, 6, 3, 4)


def pick(source, lane):
    return jnp.take_along_axis(source, lane, axis=1, mode="promise_in_bounds")


def add_up(values):
    total = values[0]
    for value in values[1:]:
        total = total + value
    return total


def split_terms(values):
    terms = []
    for number in range(SPLITS):
        term = values.astype(jnp.bfloat16).astype(jnp.float32)
        terms.append(term)
        if number + 1 < SPLITS:
            values = values - term
    return terms


def dot(left, hot):
    return lax.dot_general(
        left, hot, (((1,), (0,)), ((), ())), preferred_element_type=jnp.float32
    )


def sum_rows(values):
    for shift in (4, 2, 1):
        values = values + pltpu.roll(values, shift, 0)
    return values


def inverse_six(entry):
    lower, flipped = {}, []
    for column in range(6):
        scaled = [lower[column, inner] * flipped[inner][0] for inner in range(column)]
        value = entry(column, column)
        for inner in range(column):
            value = value - scaled[inner] * lower[column, inner]
        flipped.append((value, 1.0 / value))
        for row in range(column + 1, 6):
            value = entry(column, row)
            for inner in range(column):
                value = value - lower[row, inner] * scaled[inner]
            lower[row, column] = value * flipped[column][1]
    unit = {}
    for column in range(6):
        for row in range(column + 1, 6):
            value = -lower[row, column]
            for inner in range(column + 1, row):
                value = value - lower[row, inner] * unit[inner, column]
            unit[row, column] = value
    result = {}
    for row in range(6):
        weighted = {inner: flipped[inner][1] * unit[inner, row] for inner in range(row + 1, 6)}
        weighted[row] = flipped[row][1]
        for column in range(row + 1):
            terms = []
            for inner in range(row, 6):
                term = weighted[inner]
                terms.append(term if inner == column else term * unit[inner, column])
            result[row, column] = result[column, row] = add_up(terms)
    return result


def weigh(left, right, moments, skip=None):
    weights = {}
    for i, a in enumerate(left):
        for j, b in enumerate(right):
            if i + j != skip:
                weights.setdefault(i + j, []).append(a * b)
    return add_up([add_up(w) * moments[i] for i, w in weights.items()])


def image_of(direction):
    return [
        add_up([direction[i] for i in (j - 1, j) if 0 <= i < len(direction)])
        for j in range(len(direction) + 1)
    ]


def coefficients(moments):
    one = jnp.ones_like(moments[0])
    step, residual, direction = [], [one], [one]
    norm_now = moments[0]
    for iteration in range(ITERS - 1):
        image = image_of(direction)
        length = norm_now / weigh(direction, image, moments)
        step = [a + length * b for a, b in zip(step, direction)] + [length * direction[-1]]
        residual = [a - length * b for a, b in zip(residual, image)] + [-length * image[-1]]
        norm_next = weigh(residual, residual, moments)
        ratio = norm_next / norm_now
        direction = [a + ratio * b for a, b in zip(residual, direction)] + [residual[-1]]
        norm_now = norm_next
    return step, residual, direction, image_of(direction), norm_now


def energy_rest(direction, image, moments):
    top = len(direction) - 1
    rest = weigh(direction, image, moments, skip=2 * top + 1)
    return rest - direction[top] * image[top + 1] * moments[2 * top]


def kernel(
    sizes,
    load_hbm, prox_hbm, block_hbm, slack_hbm, dual_hbm, first_hbm, second_hbm, border_hbm,
    step_ref, residual_ref,
    load_in, prox_in, block_in, slack_in, dual_in, first_in, second_in, border_in, in_sem,
    g, hot1, hot2, hotb, span1, span2, spanb, laneb, chunkb, border_pad,
    left1, left2, left_halo, leftb, spread, spread_first, spread_pairs, spread_pairs_first,
    basis_v, basis_q, prox, inverse, diag, returned, columns,
    diag_send, diag_recv, fore_send, fore_recv, back_send, back_recv,
    early_send, early_recv, early_whole_send, early_whole_recv,
    part_send, part_recv, whole_send, whole_recv,
    diag_ssem, diag_rsem, fore_ssem, fore_rsem, back_ssem, back_rsem,
    early_ssem, early_rsem, early_whole_ssem, early_whole_rsem,
    part_ssem, part_rsem, whole_ssem, whole_rsem,
):
    nx, ny, ys, zs = sizes
    chunks = load_in.shape[0] // FIELDS
    spans = chunks * LANES // SPAN
    tiles = first_in.shape[0]
    f32, bf16 = jnp.float32, jnp.bfloat16
    gx, gy = lax.axis_index("gx"), lax.axis_index("gy")
    z_at, y_at, core = gx // (2 * ys), (gx // 2) % ys, gx % 2

    near = [((gx + dx + nx) % nx, (gy + dy + ny) % ny) for dx, dy in OFFSETS]
    real = []
    for dx, dy in OFFSETS:
        to_x, to_y = gx + dx, gy + dy
        real.append((to_x >= 0) & (to_x < nx) & (to_y >= 0) & (to_y < ny))
    part_count, whole_count = ny * ys, zs * 2
    part_near, whole_near = [], []
    for offset in range(part_count):
        other = (gy * ys + y_at + offset) % part_count
        part_near.append((z_at * 2 * ys + (other % ys) * 2 + 1 - core, other // ys))
    for offset in range(1, whole_count):
        other = (z_at * 2 + core + offset) % whole_count
        whole_near.append(((other // 2) * 2 * ys + y_at * 2 + other % 2, gy))
    barrier = pltpu.get_barrier_semaphore()
    everyone = [near[k] for k in FAR + CLOSE] + part_near + whole_near
    for device in everyone:
        pl.semaphore_signal(barrier, inc=1, device_id=device, device_id_type=MESH)

    loads = []
    for number, (source, target) in enumerate(
        (
            (second_hbm, second_in),
            (block_hbm, block_in),
            (slack_hbm, slack_in),
            (dual_hbm, dual_in),
            (first_hbm, first_in),
            (border_hbm, border_in),
            (load_hbm, load_in),
            (prox_hbm, prox_in),
        )
    ):
        loads.append(pltpu.make_async_copy(source, target, in_sem.at[number]))
        loads[-1].start()

    lane_group = lax.broadcasted_iota(jnp.int32, (1, LANES), 1) // 32
    lane_at = lax.broadcasted_iota(jnp.int32, (LANES, LANES), 1)

    def build_hot(hot, row, at):
        spot = jnp.transpose(jnp.broadcast_to(row % SPAN, (LANES, LANES)).astype(f32))
        for part in range(SPAN // LANES):
            same = spot == (lane_at + part * LANES).astype(f32)
            hot[at : at + LANES, part * LANES : (part + 1) * LANES] = jnp.where(
                same, 1.0, 0.0
            ).astype(bf16)

    def write_terms(target, values, masks):
        pieces = [jnp.where(mask, t, 0.0) for t in split_terms(values) for mask in masks]
        if (len(pieces) * values.shape[1]) % 16:
            pieces.append(jnp.zeros((values.shape[0], ROWS, LANES), f32))
        packed = jnp.concatenate(pieces, axis=1).astype(bf16)
        for s in range(values.shape[0]):
            target[0 : packed.shape[1], s * LANES : (s + 1) * LANES] = packed[s]
        return packed.shape[1]

    def read_terms(product, rows, masks):
        result = []
        for mask in range(masks):
            total = add_up(
                [
                    product[(n * masks + mask) * rows : (n * masks + mask + 1) * rows]
                    for n in range(SPLITS)
                ]
            )
            result.extend([total[:, :LANES], total[:, LANES:]])
        return result

    def arrange(slots, place_of):
        halves = [[], []]
        for k in range(8):
            place = place_of(k)
            code = jnp.where(real[k], place % 4, -1)
            halves[place // 4].append(jnp.where(lane_group == code, slots(k), 0.0))
        return [add_up(half) for half in halves]

    def reverse(k):
        return 7 - k

    def forward(k):
        return k

    def exchange(send, recv, ssem, rsem, place_of, directions=FAR + CLOSE):
        copies = []
        for k in directions:
            copies.append(
                pltpu.make_async_remote_copy(
                    src_ref=send.at[place_of(k) // 4],
                    dst_ref=recv.at[7 - k],
                    send_sem=ssem.at[k],
                    recv_sem=rsem.at[7 - k],
                    device_id=near[k],
                    device_id_type=MESH,
                )
            )
            copies[-1].start()
        return copies

    def broadcast_all(sender, receiver, ssem, rsem, devices):
        copies = []
        for number, device in enumerate(devices):
            copies.append(
                pltpu.make_async_remote_copy(
                    src_ref=sender,
                    dst_ref=receiver.at[number],
                    send_sem=ssem.at[number],
                    recv_sem=rsem.at[number],
                    device_id=device,
                    device_id_type=MESH,
                )
            )
            copies[-1].start()
        return copies

    def sent(copies):
        for copy in copies:
            copy.wait_send()

    def arrived(copies):
        for copy in copies:
            copy.wait_recv()

    spread[...] = jnp.zeros_like(spread)
    spread_first[...] = jnp.zeros_like(spread_first)
    spread_pairs[...] = jnp.zeros_like(spread_pairs)
    spread_pairs_first[...] = jnp.zeros_like(spread_pairs_first)
    loads[0].wait()
    for s in range(tiles):
        row = second_in[s : s + 1, :]
        span2[s] = jnp.broadcast_to(row // SPAN, (ROWS, LANES))
        build_hot(hot2, row, s * LANES)

    def masks_of(span, rows, wanted):
        value = span[...]
        if rows != ROWS:
            value = jnp.concatenate([value] * (rows // ROWS), axis=1)
        return [value == number for number in wanted]

    def pair_products(base, target):
        for p, (a, b) in enumerate(PAIRS):
            value = add_up([g[r * 12 + base + a] * g[r * 12 + base + b] for r in range(6)])
            target[pl.ds(p, tiles, stride=PAIR_ROWS), :] = value

    for number in (1, 2, 3):
        loads[number].wait()
    root = [jnp.sqrt(dual_in[r] / slack_in[r]) for r in range(6)]
    for r in range(6):
        for j in range(6, 12):
            g[r * 12 + j] = block_in[r * 12 + j] * root[r]
    pair_products(6, spread_pairs)
    pair_values = spread_pairs[...].reshape(tiles, PAIR_ROWS, LANES)
    rows = write_terms(left_halo, pair_values, masks_of(span2, PAIR_ROWS, [spans]))
    halves = read_terms(dot(left_halo[0:rows, :], hot2[...]), PAIR_ROWS, 1)
    for half in range(2):
        diag_send[half] = halves[half]
    pl.semaphore_wait(barrier, len(everyone))
    copies = exchange(diag_send, diag_recv, diag_ssem, diag_rsem, forward)

    rows = write_terms(left2, pair_values, masks_of(span2, PAIR_ROWS, range(spans)))
    local2 = read_terms(dot(left2[0:rows, :], hot2[...]), PAIR_ROWS, spans)
    for r in range(6):
        for j in range(6):
            g[r * 12 + j] = block_in[r * 12 + j] * root[r]
    pair_products(0, spread_pairs_first)
    loads[4].wait()
    for s in range(tiles):
        row = first_in[s : s + 1, :]
        span1[s] = jnp.broadcast_to(row // SPAN, (ROWS, LANES))
        build_hot(hot1, row, s * LANES)
    pair_values = spread_pairs_first[...].reshape(tiles, PAIR_ROWS, LANES)
    rows = write_terms(left1, pair_values, masks_of(span1, PAIR_ROWS, range(spans)))
    local1 = read_terms(dot(left1[0:rows, :], hot1[...]), PAIR_ROWS, spans)
    for c in range(chunks):
        diag[c] = local1[c] + local2[c]
    loads[5].wait()
    border_pad[...] = jnp.zeros_like(border_pad)
    border_pad[:, : border_in.shape[1]] = border_in[...]
    for half in range(2):
        row = border_pad[7 - 4 * half : 8 - 4 * half, :]
        for quarter in range(1, 4):
            place = 4 * half + quarter
            moved = pltpu.roll(border_pad[7 - place : 8 - place, :], 32 * quarter, 1)
            row = jnp.where(lane_group == quarter, moved, row)
        build_hot(hotb, row, half * LANES)
        whole = jnp.broadcast_to(row, (ROWS, LANES))
        laneb[half] = whole % LANES
        chunkb[half] = whole // LANES
        spanb[half] = whole // SPAN
    loads[6].wait()
    loads[7].wait()
    zero_rows = jnp.zeros((ROWS - FIELDS, LANES), f32)
    for c in range(chunks):
        basis_q[0, c] = jnp.concatenate(
            [load_in[pl.ds(c, FIELDS, stride=chunks), :], zero_rows], axis=0
        )
        prox[c] = jnp.concatenate(
            [prox_in[pl.ds(c, FIELDS, stride=chunks), :], zero_rows], axis=0
        )
    inverse[...] = jnp.zeros_like(inverse)
    columns[...] = jnp.zeros_like(columns)
    lane1, chunk1 = first_in[...] % LANES, first_in[...] // LANES
    lane2, chunk2 = second_in[...] % LANES, second_in[...] // LANES

    sent(copies)
    arrived(copies)
    halves = arrange(lambda k: diag_recv[k], reverse)
    for half in range(2):
        returned[half] = halves[half]
    rows = write_terms(leftb, returned[...], masks_of(spanb, PAIR_ROWS, range(spans)))
    localb = read_terms(dot(leftb[0:rows, :], hotb[...]), PAIR_ROWS, spans)
    entries = {}
    for c in range(chunks):
        spread_pairs[pl.ds(c, PAIR_ROWS, stride=ROWS), :] = diag[c] + localb[c]
    for p, (a, b) in enumerate(PAIRS):
        value = spread_pairs[p * ROWS : p * ROWS + chunks, :]
        if a == b:
            value = value + prox_in[a * chunks : (a + 1) * chunks, :]
        entries[a, b] = value
    for (a, b), value in inverse_six(lambda a, b: entries[a, b]).items():
        inverse[pl.ds(b * chunks * ROWS + a, chunks, stride=ROWS), :] = value

    def precondition(field):
        result = []
        for c in range(chunks):
            terms = []
            for b in range(FIELDS):
                at = (b * chunks + c) * ROWS
                terms.append(
                    inverse[at : at + ROWS, :]
                    * jnp.broadcast_to(field[c][b : b + 1, :], (ROWS, LANES))
                )
            result.append(add_up(terms))
        return result

    moments = jnp.zeros((1, LANES), f32)
    moment_group = lax.broadcasted_iota(jnp.int32, (1, LANES), 1) // 16

    def inner(left, right):
        value = sum_rows(add_up([left[c] * right[c] for c in range(chunks)]))[0:1]
        for shift in (64, 32, 16):
            value = value + pltpu.roll(value, shift, 1)
        return value

    def gather_fields(rows_of, lane, chunk, start, count):
        result = []
        for f in range(FIELDS):
            value = None
            for n in range(count):
                source = jnp.broadcast_to(rows_of(f, n), (tiles, LANES))
                piece = pick(source, lane)
                if value is None:
                    value = piece if start == 0 else jnp.where(chunk == start, piece, 0.0)
                else:
                    value = jnp.where(chunk == start + n, piece, value)
            result.append(value)
        return result

    q_now = [basis_q[0, c] for c in range(chunks)]
    v_now = precondition(q_now)
    late = []
    for k in range(ITERS):
        for c in range(chunks):
            basis_v[k, c] = v_now[c]
        ends = []
        for half in range(2):
            value = pick(v_now[0], laneb[half])
            for c in range(1, chunks):
                value = jnp.where(chunkb[half] == c, pick(v_now[c], laneb[half]), value)
            ends.append(value)
            fore_send[k, half] = value
        fore_refs = (fore_send.at[k], fore_recv.at[k], fore_ssem.at[k], fore_rsem.at[k], reverse)
        back_refs = (back_send.at[k], back_recv.at[k], back_ssem.at[k], back_rsem.at[k], forward)
        fore = exchange(*fore_refs, FAR)
        u1 = gather_fields(lambda f, n: basis_v[k, n, f : f + 1, :], lane1, chunk1, 0, chunks)
        strain = [add_up([g[r * 12 + j] * u1[j] for j in range(6)]) for r in range(6)]
        for j in range(6):
            value = add_up([g[r * 12 + 6 + j] * strain[r] for r in range(6)])
            spread[pl.ds(j, tiles, stride=ROWS), :] = value
        pulls = spread[...].reshape(tiles, ROWS, LANES)
        rows = write_terms(left_halo, pulls, masks_of(span2, ROWS, [spans]))
        halves = read_terms(dot(left_halo[0:rows, :], hot2[...]), ROWS, 1)
        for half in range(2):
            back_send[k, half] = halves[half]
        back = exchange(*back_refs, FAR)
        fore = fore + exchange(*fore_refs, CLOSE)
        back = back + exchange(*back_refs, CLOSE)
        norm = inner(v_now, q_now)
        moments = jnp.where(moment_group == 2 * k, norm, moments)
        if k == ITERS - 1:
            early_send[...] = moments
            early = broadcast_all(early_send, early_recv, early_ssem, early_rsem, part_near)
        u2 = gather_fields(lambda f, n: basis_v[k, n, f : f + 1, :], lane2, chunk2, 0, chunks)
        here = chunk2 < chunks
        u2 = [jnp.where(here, value, 0.0) for value in u2]
        strain = [
            strain[r] + add_up([g[r * 12 + 6 + j] * u2[j] for j in range(6)]) for r in range(6)
        ]
        for j in range(6):
            value = add_up([g[r * 12 + 6 + j] * strain[r] for r in range(6)])
            spread[pl.ds(j, tiles, stride=ROWS), :] = value
        pulls = spread[...].reshape(tiles, ROWS, LANES)
        rows = write_terms(left2, pulls, masks_of(span2, ROWS, range(spans)))
        image = read_terms(dot(left2[0:rows, :], hot2[...]), ROWS, spans)
        image = [image[c] + prox[c] * v_now[c] - q_now[c] for c in range(chunks)]
        pushes = [add_up([g[r * 12 + j] * strain[r] for r in range(6)]) for j in range(6)]
        if k == 0:
            for p, (a, b) in enumerate(PAIRS):
                for half in range(2):
                    row = returned[half, p : p + 1, :]
                    columns[b, half, a : a + 1, :] = row
                    if a != b:
                        columns[a, half, b : b + 1, :] = row
        pulled = []
        for half in range(2):
            pulled.append(
                add_up(
                    [
                        columns[b, half]
                        * jnp.broadcast_to(ends[half][b : b + 1, :], (ROWS, LANES))
                        for b in range(FIELDS)
                    ]
                )
            )
        sent(late)
        sent(fore)
        arrived(fore)
        beyond = arrange(lambda s: fore_recv[k, s], forward)
        u2 = gather_fields(lambda f, n: beyond[n][f : f + 1, :], lane2, chunk2, chunks, 2)
        more = [
            add_up([g[r * 12 + 6 + j] * u2[j] for j in range(6)]) for r in range(6)
        ]
        for j in range(6):
            value = pushes[j] + add_up([g[r * 12 + j] * more[r] for r in range(6)])
            spread_first[pl.ds(j, tiles, stride=ROWS), :] = value
        if k == ITERS - 1:
            energy = add_up([(strain[r] + more[r]) * (strain[r] + more[r]) for r in range(6)])
            energy = add_up([energy[t : t + ROWS] for t in range(0, tiles, ROWS)])
            energy = energy + add_up([prox[c] * v_now[c] * v_now[c] for c in range(chunks)])
            part_send[...] = sum_rows(energy)[0:1]
            part = broadcast_all(part_send, part_recv, part_ssem, part_rsem, part_near)
        values = spread_first[...].reshape(tiles, ROWS, LANES)
        rows = write_terms(left1, values, masks_of(span1, ROWS, range(spans)))
        pushed = read_terms(dot(left1[0:rows, :], hot1[...]), ROWS, spans)
        image = [image[c] + pushed[c] for c in range(chunks)]
        arrived(back)
        late = back
        halves = arrange(lambda s: back_recv[k, s], reverse)
        values = jnp.concatenate([(halves[h] + pulled[h])[None] for h in range(2)], axis=0)
        rows = write_terms(leftb, values, masks_of(spanb, ROWS, range(spans)))
        added = read_terms(dot(leftb[0:rows, :], hotb[...]), ROWS, spans)
        q_next = [image[c] + added[c] for c in range(chunks)]
        for c in range(chunks):
            basis_q[k + 1, c] = q_next[c]
        if k < ITERS - 1:
            v_next = precondition(q_next)
            moments = jnp.where(moment_group == 2 * k + 1, inner(v_now, q_next), moments)
            q_now, v_now = q_next, v_next

    sent(early)
    arrived(early)
    early_whole_send[...] = add_up([early_recv[n] for n in range(len(part_near))])
    early = broadcast_all(
        early_whole_send, early_whole_recv, early_whole_ssem, early_whole_rsem, whole_near
    )
    sent(late)
    sent(part)
    arrived(part)
    whole_send[...] = add_up([part_recv[n] for n in range(len(part_near))])
    whole = broadcast_all(whole_send, whole_recv, whole_ssem, whole_rsem, whole_near)
    sent(early)
    arrived(early)
    total = early_whole_send[...] + add_up([early_whole_recv[n] for n in range(len(whole_near))])
    row_at = lax.broadcasted_iota(jnp.int32, (ROWS, LANES), 0)
    group_at = lax.broadcasted_iota(jnp.int32, (ROWS, LANES), 1) // 16
    total = jnp.where(row_at == group_at, jnp.broadcast_to(total, (ROWS, LANES)), 0.0)
    sums = jnp.sum(total, axis=1, keepdims=True)
    moments = [jnp.broadcast_to(sums[i : i + 1, :], (ROWS, LANES)) for i in range(2 * ITERS - 1)]
    step, residual, direction, image, norm_now = coefficients(moments)
    rest = energy_rest(direction, image, moments)
    before, ahead, left, drop = [], [], [], []
    for c in range(chunks):
        before.append(add_up([step[j] * basis_v[j, c] for j in range(ITERS - 1)]))
        ahead.append(add_up([direction[j] * basis_v[j, c] for j in range(ITERS)]))
        left.append(add_up([residual[j] * basis_q[j, c] for j in range(ITERS)]))
        drop.append(add_up([image[j] * basis_q[j, c] for j in range(ITERS + 1)]))
    sent(whole)
    arrived(whole)
    total = whole_send[...] + add_up([whole_recv[n] for n in range(len(whole_near))])
    energy = jnp.broadcast_to(jnp.sum(total, axis=1, keepdims=True), (ROWS, LANES))
    length = norm_now / (rest + direction[-1] * image[-1] * energy)
    for c in range(chunks):
        rows = pl.ds(c, FIELDS, stride=chunks)
        step_ref[0, rows, :] = before[c][0:FIELDS]
        step_ref[1, rows, :] = (length * ahead[c])[0:FIELDS]
        residual_ref[0, rows, :] = left[c][0:FIELDS]
        residual_ref[1, rows, :] = (-length * drop[c])[0:FIELDS]


def local(mesh_shape, body_load, proximal, contact_blocks, slacks, dual_rows, first_body, second_body, border_bodies):
    nx, ny = mesh_shape
    ys = 4 if nx % 8 == 0 else 1
    zs = nx // (2 * ys)
    bodies, contacts = body_load.shape[3], contact_blocks.shape[4]
    chunks, tiles, spans = bodies // LANES, contacts // LANES, bodies // SPAN
    f32, bf16, i32 = jnp.float32, jnp.bfloat16, jnp.int32
    vmem = pltpu.VMEM
    dma = pltpu.SemaphoreType.DMA
    parts, wholes = ny * ys, 2 * zs - 1
    pair_rows = PAIR_ROWS * SPLITS
    operands = (
        body_load.reshape(FIELDS * chunks, LANES),
        proximal.reshape(FIELDS * chunks, LANES),
        contact_blocks.reshape(12 * FIELDS, tiles, LANES),
        slacks.reshape(FIELDS, tiles, LANES),
        dual_rows.reshape(FIELDS, tiles, LANES),
        first_body.reshape(tiles, LANES),
        second_body.reshape(tiles, LANES),
        border_bodies.reshape(border_bodies.shape[2:]),
    )
    scratch = [vmem(a.shape, a.dtype) for a in operands] + [
        dma((8,)),
        vmem((12 * FIELDS, tiles, LANES), f32),
        vmem((contacts, SPAN), bf16),
        vmem((contacts, SPAN), bf16),
        vmem((2 * LANES, SPAN), bf16),
        vmem((tiles, ROWS, LANES), i32),
        vmem((tiles, ROWS, LANES), i32),
        vmem((2, ROWS, LANES), i32),
        vmem((2, ROWS, LANES), i32),
        vmem((2, ROWS, LANES), i32),
        vmem((ROWS, LANES), i32),
        vmem((pair_rows * spans, contacts), bf16),
        vmem((pair_rows * spans, contacts), bf16),
        vmem((pair_rows + ROWS, contacts), bf16),
        vmem((pair_rows * spans, 2 * LANES), bf16),
        vmem((tiles * ROWS, LANES), f32),
        vmem((tiles * ROWS, LANES), f32),
        vmem((tiles * PAIR_ROWS, LANES), f32),
        vmem((tiles * PAIR_ROWS, LANES), f32),
        vmem((ITERS, chunks, ROWS, LANES), f32),
        vmem((ITERS + 1, chunks, ROWS, LANES), f32),
        vmem((chunks, ROWS, LANES), f32),
        vmem((FIELDS * chunks * ROWS, LANES), f32),
        vmem((chunks, PAIR_ROWS, LANES), f32),
        vmem((2, PAIR_ROWS, LANES), f32),
        vmem((FIELDS, 2, ROWS, LANES), f32),
        vmem((2, PAIR_ROWS, LANES), f32),
        vmem((8, PAIR_ROWS, LANES), f32),
        vmem((ITERS, 2, ROWS, LANES), f32),
        vmem((ITERS, 8, ROWS, LANES), f32),
        vmem((ITERS, 2, ROWS, LANES), f32),
        vmem((ITERS, 8, ROWS, LANES), f32),
        vmem((1, LANES), f32),
        vmem((parts, 1, LANES), f32),
        vmem((1, LANES), f32),
        vmem((wholes, 1, LANES), f32),
        vmem((1, LANES), f32),
        vmem((parts, 1, LANES), f32),
        vmem((1, LANES), f32),
        vmem((wholes, 1, LANES), f32),
        dma((8,)),
        dma((8,)),
        dma((ITERS, 8)),
        dma((ITERS, 8)),
        dma((ITERS, 8)),
        dma((ITERS, 8)),
        dma((parts,)),
        dma((parts,)),
        dma((wholes,)),
        dma((wholes,)),
        dma((parts,)),
        dma((parts,)),
        dma((wholes,)),
        dma((wholes,)),
    ]
    step, residual = pl.pallas_call(
        functools.partial(kernel, (nx, ny, ys, zs)),
        out_shape=[jax.ShapeDtypeStruct((2, FIELDS * chunks, LANES), f32)] * 2,
        in_specs=[pl.BlockSpec(memory_space=pltpu.HBM)] * 8,
        out_specs=[pl.BlockSpec(memory_space=pltpu.VMEM)] * 2,
        scratch_shapes=scratch,
        compiler_params=pltpu.CompilerParams(
            collective_id=0, has_side_effects=True, vmem_limit_bytes=56 * 1024 * 1024
        ),
    )(*operands)
    step, residual = step[0] + step[1], residual[0] + residual[1]
    return step.reshape(body_load.shape), residual.reshape(body_load.shape)


def solution(mesh):
    return jax.shard_map(
        functools.partial(local, (mesh.shape["gx"], mesh.shape["gy"])),
        mesh=mesh,
        in_specs=(
            P("gx", "gy", None, None),
            P("gx", "gy", None, None),
            P("gx", "gy", None, None, None),
            P("gx", "gy", None, None),
            P("gx", "gy", None, None),
            P("gx", "gy", None),
            P("gx", "gy", None),
            P("gx", "gy", None, None),
        ),
        out_specs=(P("gx", "gy", None, None), P("gx", "gy", None, None)),
        check_vma=False,
    )
```

```python
import functools

import jax
import jax.numpy as jnp
from jax import lax
from jax.experimental import pallas as pl
from jax.experimental.pallas import tpu as pltpu
from jax.sharding import PartitionSpec as P

ITERS = 4
LANES = 128
ROWS = 8
SPAN = 256
HALO_SPANS = 2 * LANES // SPAN
SPLITS = 3
LOOP_SPLITS = 3
FIELDS = 6
PAIRS = [(a, b) for a in range(FIELDS) for b in range(a, FIELDS)]
PAIR_ROWS = 24
MESH = pl.DeviceIdType.MESH
OFFSETS = ((-1, -1), (-1, 0), (-1, 1), (0, -1), (0, 1), (1, -1), (1, 0), (1, 1))
FAR = (0, 2, 5, 7)
CLOSE = (1, 6, 3, 4)


def pick(source, lane):
    return jnp.take_along_axis(source, lane, axis=1, mode="promise_in_bounds")


def add_up(values):
    while len(values) > 1:
        pairs = [a + b for a, b in zip(values[::2], values[1::2])]
        values = pairs + values[len(pairs) * 2 :]
    return values[0]


def split_terms(values, splits):
    terms = []
    for number in range(splits):
        term = values.astype(jnp.bfloat16).astype(jnp.float32)
        terms.append(term)
        if number + 1 < splits:
            values = values - term
    return terms


def dot(left, hot):
    return lax.dot_general(
        left, hot, (((1,), (0,)), ((), ())), preferred_element_type=jnp.float32
    )


def sum_rows(values):
    for shift in (4, 2, 1):
        values = values + pltpu.roll(values, shift, 0)
    return values


def inverse_six(entry):
    lower, flipped = {}, []
    for column in range(6):
        scaled = [lower[column, inner] * flipped[inner][0] for inner in range(column)]
        value = entry(column, column)
        for inner in range(column):
            value = value - scaled[inner] * lower[column, inner]
        flipped.append((value, 1.0 / value))
        for row in range(column + 1, 6):
            value = entry(column, row)
            for inner in range(column):
                value = value - lower[row, inner] * scaled[inner]
            lower[row, column] = value * flipped[column][1]
    unit = {}
    for column in range(6):
        for row in range(column + 1, 6):
            value = -lower[row, column]
            for inner in range(column + 1, row):
                value = value - lower[row, inner] * unit[inner, column]
            unit[row, column] = value
    result = {}
    for row in range(6):
        weighted = {inner: flipped[inner][1] * unit[inner, row] for inner in range(row + 1, 6)}
        weighted[row] = flipped[row][1]
        for column in range(row + 1):
            terms = []
            for inner in range(row, 6):
                term = weighted[inner]
                terms.append(term if inner == column else term * unit[inner, column])
            result[row, column] = result[column, row] = add_up(terms)
    return result


def weigh(left, right, moments, skip=None):
    weights = {}
    for i, a in enumerate(left):
        for j, b in enumerate(right):
            if i + j != skip:
                weights.setdefault(i + j, []).append(a * b)
    return add_up([add_up(w) * moments[i] for i, w in weights.items()])


def image_of(direction):
    return [
        add_up([direction[i] for i in (j - 1, j) if 0 <= i < len(direction)])
        for j in range(len(direction) + 1)
    ]


def coefficients(moments):
    one = jnp.ones_like(moments[0])
    step, residual, direction = [], [one], [one]
    norm_now = moments[0]
    for iteration in range(ITERS - 1):
        image = image_of(direction)
        length = norm_now / weigh(direction, image, moments)
        step = [a + length * b for a, b in zip(step, direction)] + [length * direction[-1]]
        residual = [a - length * b for a, b in zip(residual, image)] + [-length * image[-1]]
        norm_next = weigh(residual, residual, moments)
        ratio = norm_next / norm_now
        direction = [a + ratio * b for a, b in zip(residual, direction)] + [residual[-1]]
        norm_now = norm_next
    return step, residual, direction, image_of(direction), norm_now


def energy_rest(direction, image, moments):
    top = len(direction) - 1
    rest = weigh(direction, image, moments, skip=2 * top + 1)
    return rest - direction[top] * image[top + 1] * moments[2 * top]


def kernel(
    sizes,
    load_hbm, prox_hbm, block_hbm, slack_hbm, dual_hbm, first_hbm, second_hbm, border_hbm,
    step_ref, residual_ref,
    load_in, prox_in, block_in, slack_in, dual_in, first_in, second_in, border_in, in_sem,
    g, cross, hot1, hot2, hotb, span1, span2, spanb, laneb, chunkb, border_pad,
    left1, left2, left_halo, leftb, spread, spread_first, spread_pairs, spread_pairs_first,
    basis_v, basis_q, prox, inverse, diag, returned, columns,
    diag_send, diag_recv, fore_send, fore_recv, back_send, back_recv,
    early_send, early_recv, early_whole_send, early_whole_recv,
    part_send, part_recv, whole_send, whole_recv,
    diag_ssem, diag_rsem, fore_ssem, fore_rsem, back_ssem, back_rsem,
    early_ssem, early_rsem, early_whole_ssem, early_whole_rsem,
    part_ssem, part_rsem, whole_ssem, whole_rsem,
):
    nx, ny, ys, zs = sizes
    chunks = load_in.shape[0] // FIELDS
    spans = chunks * LANES // SPAN
    tiles = first_in.shape[0]
    HALO = range(spans, spans + HALO_SPANS)
    f32, bf16 = jnp.float32, jnp.bfloat16
    gx, gy = lax.axis_index("gx"), lax.axis_index("gy")
    z_at, y_at, core = gx // (2 * ys), (gx // 2) % ys, gx % 2

    near = [((gx + dx + nx) % nx, (gy + dy + ny) % ny) for dx, dy in OFFSETS]
    real = []
    for dx, dy in OFFSETS:
        to_x, to_y = gx + dx, gy + dy
        real.append((to_x >= 0) & (to_x < nx) & (to_y >= 0) & (to_y < ny))
    part_count, whole_count = ny * ys, zs * 2
    part_near, whole_near = [], []
    for offset in range(part_count):
        other = (gy * ys + y_at + offset) % part_count
        part_near.append((z_at * 2 * ys + (other % ys) * 2 + 1 - core, other // ys))
    for offset in range(1, whole_count):
        other = (z_at * 2 + core + offset) % whole_count
        whole_near.append(((other // 2) * 2 * ys + y_at * 2 + other % 2, gy))
    barrier = pltpu.get_barrier_semaphore()
    everyone = [near[k] for k in FAR + CLOSE] + part_near + whole_near
    for device in everyone:
        pl.semaphore_signal(barrier, inc=1, device_id=device, device_id_type=MESH)

    loads = []
    for number, (source, target) in enumerate(
        (
            (second_hbm, second_in),
            (block_hbm, block_in),
            (slack_hbm, slack_in),
            (dual_hbm, dual_in),
            (first_hbm, first_in),
            (border_hbm, border_in),
            (load_hbm, load_in),
            (prox_hbm, prox_in),
        )
    ):
        loads.append(pltpu.make_async_copy(source, target, in_sem.at[number]))
        loads[-1].start()

    lane_group = lax.broadcasted_iota(jnp.int32, (1, LANES), 1) // 32
    lane_at = lax.broadcasted_iota(jnp.int32, (LANES, LANES), 1)

    def build_hot(hot, row, at):
        spot = jnp.transpose(jnp.broadcast_to(row % SPAN, (LANES, LANES)).astype(f32))
        for part in range(SPAN // LANES):
            same = spot == (lane_at + part * LANES).astype(f32)
            hot[at : at + LANES, part * LANES : (part + 1) * LANES] = jnp.where(
                same, 1.0, 0.0
            ).astype(bf16)

    def write_terms(target, values, masks, splits):
        pieces = [jnp.where(mask, t, 0.0) for t in split_terms(values, splits) for mask in masks]
        if (len(pieces) * values.shape[1]) % 16:
            pieces.append(jnp.zeros((values.shape[0], ROWS, LANES), f32))
        packed = jnp.concatenate(pieces, axis=1).astype(bf16)
        for s in range(values.shape[0]):
            target[0 : packed.shape[1], s * LANES : (s + 1) * LANES] = packed[s]
        return packed.shape[1]

    def read_terms(product, rows, masks, splits):
        result = []
        for mask in range(masks):
            total = add_up(
                [
                    product[(n * masks + mask) * rows : (n * masks + mask + 1) * rows]
                    for n in range(splits)
                ]
            )
            result.extend([total[:, at : at + LANES] for at in range(0, SPAN, LANES)])
        return result

    def arrange(slots, place_of):
        halves = [[], []]
        for k in range(8):
            place = place_of(k)
            code = jnp.where(real[k], place % 4, -1)
            halves[place // 4].append(jnp.where(lane_group == code, slots(k), 0.0))
        return [add_up(half) for half in halves]

    def reverse(k):
        return 7 - k

    def forward(k):
        return k

    def exchange(send, recv, ssem, rsem, place_of, directions=FAR + CLOSE):
        copies = []
        for k in directions:
            copies.append(
                pltpu.make_async_remote_copy(
                    src_ref=send.at[place_of(k) // 4],
                    dst_ref=recv.at[7 - k],
                    send_sem=ssem.at[k],
                    recv_sem=rsem.at[7 - k],
                    device_id=near[k],
                    device_id_type=MESH,
                )
            )
            copies[-1].start()
        return copies

    def broadcast_all(sender, receiver, ssem, rsem, devices):
        copies = []
        for number, device in enumerate(devices):
            copies.append(
                pltpu.make_async_remote_copy(
                    src_ref=sender,
                    dst_ref=receiver.at[number],
                    send_sem=ssem.at[number],
                    recv_sem=rsem.at[number],
                    device_id=device,
                    device_id_type=MESH,
                )
            )
            copies[-1].start()
        return copies

    def sent(copies):
        for copy in copies:
            copy.wait_send()

    def arrived(copies):
        for copy in copies:
            copy.wait_recv()

    spread[...] = jnp.zeros_like(spread)
    spread_first[...] = jnp.zeros_like(spread_first)
    spread_pairs[...] = jnp.zeros_like(spread_pairs)
    spread_pairs_first[...] = jnp.zeros_like(spread_pairs_first)
    loads[0].wait()
    for s in range(tiles):
        row = second_in[s : s + 1, :]
        span2[s] = jnp.broadcast_to(row // SPAN, (ROWS, LANES))
        build_hot(hot2, row, s * LANES)

    def masks_of(span, rows, wanted):
        value = span[...]
        if rows != ROWS:
            value = jnp.concatenate([value] * (rows // ROWS), axis=1)
        return [value == number for number in wanted]

    def pair_products(base, target):
        for p, (a, b) in enumerate(PAIRS):
            value = add_up([g[r * 12 + base + a] * g[r * 12 + base + b] for r in range(6)])
            target[pl.ds(p, tiles, stride=PAIR_ROWS), :] = value

    for number in (1, 2, 3):
        loads[number].wait()
    root = [jnp.sqrt(dual_in[r] / slack_in[r]) for r in range(6)]
    for r in range(6):
        for j in range(6, 12):
            g[r * 12 + j] = block_in[r * 12 + j] * root[r]
    pair_products(6, spread_pairs)
    pair_values = spread_pairs[...].reshape(tiles, PAIR_ROWS, LANES)
    rows = write_terms(left_halo, pair_values, masks_of(span2, PAIR_ROWS, HALO), SPLITS)
    halves = read_terms(dot(left_halo[0:rows, :], hot2[...]), PAIR_ROWS, HALO_SPANS, SPLITS)
    for half in range(2):
        diag_send[half] = halves[half]
    pl.semaphore_wait(barrier, len(everyone))
    copies = exchange(diag_send, diag_recv, diag_ssem, diag_rsem, forward)

    rows = write_terms(left2, pair_values, masks_of(span2, PAIR_ROWS, range(spans)), SPLITS)
    local2 = read_terms(dot(left2[0:rows, :], hot2[...]), PAIR_ROWS, spans, SPLITS)
    for r in range(6):
        for j in range(6):
            g[r * 12 + j] = block_in[r * 12 + j] * root[r]
    pair_products(0, spread_pairs_first)
    loads[4].wait()
    for s in range(tiles):
        row = first_in[s : s + 1, :]
        span1[s] = jnp.broadcast_to(row // SPAN, (ROWS, LANES))
        build_hot(hot1, row, s * LANES)
    for j in range(6):
        for a in range(6):
            cross[j * 6 + a] = add_up([g[r * 12 + 6 + j] * g[r * 12 + a] for r in range(6)])
    pair_values = spread_pairs_first[...].reshape(tiles, PAIR_ROWS, LANES)
    rows = write_terms(left1, pair_values, masks_of(span1, PAIR_ROWS, range(spans)), SPLITS)
    local1 = read_terms(dot(left1[0:rows, :], hot1[...]), PAIR_ROWS, spans, SPLITS)
    for c in range(chunks):
        diag[c] = local1[c] + local2[c]
    loads[5].wait()
    border_pad[...] = jnp.zeros_like(border_pad)
    border_pad[:, : border_in.shape[1]] = border_in[...]
    for half in range(2):
        row = border_pad[7 - 4 * half : 8 - 4 * half, :]
        for quarter in range(1, 4):
            place = 4 * half + quarter
            moved = pltpu.roll(border_pad[7 - place : 8 - place, :], 32 * quarter, 1)
            row = jnp.where(lane_group == quarter, moved, row)
        build_hot(hotb, row, half * LANES)
        whole = jnp.broadcast_to(row, (ROWS, LANES))
        laneb[half] = whole % LANES
        chunkb[half] = whole // LANES
        spanb[half] = whole // SPAN
    loads[6].wait()
    loads[7].wait()
    zero_rows = jnp.zeros((ROWS - FIELDS, LANES), f32)
    for c in range(chunks):
        basis_q[0, c] = jnp.concatenate(
            [load_in[pl.ds(c, FIELDS, stride=chunks), :], zero_rows], axis=0
        )
        prox[c] = jnp.concatenate(
            [prox_in[pl.ds(c, FIELDS, stride=chunks), :], zero_rows], axis=0
        )
    inverse[...] = jnp.zeros_like(inverse)
    columns[...] = jnp.zeros_like(columns)
    lane1, chunk1 = first_in[...] % LANES, first_in[...] // LANES
    lane2, chunk2 = second_in[...] % LANES, second_in[...] // LANES

    sent(copies)
    arrived(copies)
    halves = arrange(lambda k: diag_recv[k], reverse)
    for half in range(2):
        returned[half] = halves[half]
    rows = write_terms(leftb, returned[...], masks_of(spanb, PAIR_ROWS, range(spans)), SPLITS)
    localb = read_terms(dot(leftb[0:rows, :], hotb[...]), PAIR_ROWS, spans, SPLITS)
    entries = {}
    for c in range(chunks):
        spread_pairs[pl.ds(c, PAIR_ROWS, stride=ROWS), :] = diag[c] + localb[c]
    for p, (a, b) in enumerate(PAIRS):
        value = spread_pairs[p * ROWS : p * ROWS + chunks, :]
        if a == b:
            value = value + prox_in[a * chunks : (a + 1) * chunks, :]
        entries[a, b] = value
    for (a, b), value in inverse_six(lambda a, b: entries[a, b]).items():
        inverse[pl.ds(b * chunks * ROWS + a, chunks, stride=ROWS), :] = value

    def precondition(field):
        result = []
        for c in range(chunks):
            terms = []
            for b in range(FIELDS):
                at = (b * chunks + c) * ROWS
                terms.append(
                    inverse[at : at + ROWS, :]
                    * jnp.broadcast_to(field[c][b : b + 1, :], (ROWS, LANES))
                )
            result.append(add_up(terms))
        return result

    moments = jnp.zeros((1, LANES), f32)
    moment_group = lax.broadcasted_iota(jnp.int32, (1, LANES), 1) // 16

    def inner(left, right):
        value = sum_rows(add_up([left[c] * right[c] for c in range(chunks)]))[0:1]
        for shift in (64, 32, 16):
            value = value + pltpu.roll(value, shift, 1)
        return value

    def gather_fields(rows_of, lane, chunk, start, count):
        result = []
        for f in range(FIELDS):
            value = None
            for n in range(count):
                source = jnp.broadcast_to(rows_of(f, n), (tiles, LANES))
                piece = pick(source, lane)
                if value is None:
                    value = piece if start == 0 else jnp.where(chunk == start, piece, 0.0)
                else:
                    value = jnp.where(chunk == start + n, piece, value)
            result.append(value)
        return result

    q_now = [basis_q[0, c] for c in range(chunks)]
    v_now = precondition(q_now)
    late = []
    for k in range(ITERS):
        for c in range(chunks):
            basis_v[k, c] = v_now[c]
        ends = []
        for half in range(2):
            value = pick(v_now[0], laneb[half])
            for c in range(1, chunks):
                value = jnp.where(chunkb[half] == c, pick(v_now[c], laneb[half]), value)
            ends.append(value)
            fore_send[k, half] = value
        fore_refs = (fore_send.at[k], fore_recv.at[k], fore_ssem.at[k], fore_rsem.at[k], reverse)
        back_refs = (back_send.at[k], back_recv.at[k], back_ssem.at[k], back_rsem.at[k], forward)
        fore = exchange(*fore_refs, FAR)
        u1 = gather_fields(lambda f, n: basis_v[k, n, f : f + 1, :], lane1, chunk1, 0, chunks)
        for j in range(6):
            value = add_up([cross[j * 6 + a] * u1[a] for a in range(6)])
            spread[pl.ds(j, tiles, stride=ROWS), :] = value
        pulls = spread[...].reshape(tiles, ROWS, LANES)
        rows = write_terms(left_halo, pulls, masks_of(span2, ROWS, HALO), LOOP_SPLITS)
        halves = read_terms(dot(left_halo[0:rows, :], hot2[...]), ROWS, HALO_SPANS, LOOP_SPLITS)
        for half in range(2):
            back_send[k, half] = halves[half]
        back = exchange(*back_refs, FAR)
        fore = fore + exchange(*fore_refs, CLOSE)
        back = back + exchange(*back_refs, CLOSE)
        norm = inner(v_now, q_now)
        moments = jnp.where(moment_group == 2 * k, norm, moments)
        if k == ITERS - 1:
            early_send[...] = moments
            early = broadcast_all(early_send, early_recv, early_ssem, early_rsem, part_near)
        u2 = gather_fields(lambda f, n: basis_v[k, n, f : f + 1, :], lane2, chunk2, 0, chunks)
        here = chunk2 < chunks
        u2 = [jnp.where(here, value, 0.0) for value in u2]
        strain = [
            add_up(
                [g[r * 12 + j] * u1[j] for j in range(6)]
                + [g[r * 12 + 6 + j] * u2[j] for j in range(6)]
            )
            for r in range(6)
        ]
        for j in range(6):
            value = add_up([g[r * 12 + 6 + j] * strain[r] for r in range(6)])
            spread[pl.ds(j, tiles, stride=ROWS), :] = value
        pulls = spread[...].reshape(tiles, ROWS, LANES)
        rows = write_terms(left2, pulls, masks_of(span2, ROWS, range(spans)), LOOP_SPLITS)
        image = read_terms(dot(left2[0:rows, :], hot2[...]), ROWS, spans, LOOP_SPLITS)
        image = [image[c] + prox[c] * v_now[c] - q_now[c] for c in range(chunks)]
        pushes = [add_up([g[r * 12 + j] * strain[r] for r in range(6)]) for j in range(6)]
        if k == 0:
            for p, (a, b) in enumerate(PAIRS):
                for half in range(2):
                    row = returned[half, p : p + 1, :]
                    columns[b, half, a : a + 1, :] = row
                    if a != b:
                        columns[a, half, b : b + 1, :] = row
        pulled = []
        for half in range(2):
            pulled.append(
                add_up(
                    [
                        columns[b, half]
                        * jnp.broadcast_to(ends[half][b : b + 1, :], (ROWS, LANES))
                        for b in range(FIELDS)
                    ]
                )
            )
        sent(late)
        sent(fore)
        arrived(fore)
        beyond = arrange(lambda s: fore_recv[k, s], forward)
        u2 = gather_fields(lambda f, n: beyond[n][f : f + 1, :], lane2, chunk2, chunks, 2)
        for a in range(6):
            value = pushes[a] + add_up([cross[j * 6 + a] * u2[j] for j in range(6)])
            spread_first[pl.ds(a, tiles, stride=ROWS), :] = value
        if k == ITERS - 1:
            more = [add_up([g[r * 12 + 6 + j] * u2[j] for j in range(6)]) for r in range(6)]
            energy = add_up([(strain[r] + more[r]) * (strain[r] + more[r]) for r in range(6)])
            energy = add_up([energy[t : t + ROWS] for t in range(0, tiles, ROWS)])
            energy = energy + add_up([prox[c] * v_now[c] * v_now[c] for c in range(chunks)])
            part_send[...] = sum_rows(energy)[0:1]
            part = broadcast_all(part_send, part_recv, part_ssem, part_rsem, part_near)
        values = spread_first[...].reshape(tiles, ROWS, LANES)
        rows = write_terms(left1, values, masks_of(span1, ROWS, range(spans)), LOOP_SPLITS)
        pushed = read_terms(dot(left1[0:rows, :], hot1[...]), ROWS, spans, LOOP_SPLITS)
        image = [image[c] + pushed[c] for c in range(chunks)]
        arrived(back)
        late = back
        halves = arrange(lambda s: back_recv[k, s], reverse)
        values = jnp.concatenate([(halves[h] + pulled[h])[None] for h in range(2)], axis=0)
        rows = write_terms(leftb, values, masks_of(spanb, ROWS, range(spans)), LOOP_SPLITS)
        added = read_terms(dot(leftb[0:rows, :], hotb[...]), ROWS, spans, LOOP_SPLITS)
        q_next = [image[c] + added[c] for c in range(chunks)]
        for c in range(chunks):
            basis_q[k + 1, c] = q_next[c]
        if k < ITERS - 1:
            v_next = precondition(q_next)
            moments = jnp.where(moment_group == 2 * k + 1, inner(v_now, q_next), moments)
            q_now, v_now = q_next, v_next

    sent(early)
    arrived(early)
    early_whole_send[...] = add_up([early_recv[n] for n in range(len(part_near))])
    early = broadcast_all(
        early_whole_send, early_whole_recv, early_whole_ssem, early_whole_rsem, whole_near
    )
    sent(late)
    sent(part)
    arrived(part)
    whole_send[...] = add_up([part_recv[n] for n in range(len(part_near))])
    whole = broadcast_all(whole_send, whole_recv, whole_ssem, whole_rsem, whole_near)
    sent(early)
    arrived(early)
    total = early_whole_send[...] + add_up([early_whole_recv[n] for n in range(len(whole_near))])
    row_at = lax.broadcasted_iota(jnp.int32, (ROWS, LANES), 0)
    group_at = lax.broadcasted_iota(jnp.int32, (ROWS, LANES), 1) // 16
    total = jnp.where(row_at == group_at, jnp.broadcast_to(total, (ROWS, LANES)), 0.0)
    sums = jnp.sum(total, axis=1, keepdims=True)
    moments = [jnp.broadcast_to(sums[i : i + 1, :], (ROWS, LANES)) for i in range(2 * ITERS - 1)]
    step, residual, direction, image, norm_now = coefficients(moments)
    rest = energy_rest(direction, image, moments)
    before, ahead, left, drop = [], [], [], []
    for c in range(chunks):
        before.append(add_up([step[j] * basis_v[j, c] for j in range(ITERS - 1)]))
        ahead.append(add_up([direction[j] * basis_v[j, c] for j in range(ITERS)]))
        left.append(add_up([residual[j] * basis_q[j, c] for j in range(ITERS)]))
        drop.append(add_up([image[j] * basis_q[j, c] for j in range(ITERS + 1)]))
    sent(whole)
    arrived(whole)
    total = whole_send[...] + add_up([whole_recv[n] for n in range(len(whole_near))])
    energy = jnp.broadcast_to(jnp.sum(total, axis=1, keepdims=True), (ROWS, LANES))
    length = norm_now / (rest + direction[-1] * image[-1] * energy)
    for c in range(chunks):
        rows = pl.ds(c, FIELDS, stride=chunks)
        step_ref[0, rows, :] = before[c][0:FIELDS]
        step_ref[1, rows, :] = (length * ahead[c])[0:FIELDS]
        residual_ref[0, rows, :] = left[c][0:FIELDS]
        residual_ref[1, rows, :] = (-length * drop[c])[0:FIELDS]


def local(mesh_shape, body_load, proximal, contact_blocks, slacks, dual_rows, first_body, second_body, border_bodies):
    nx, ny = mesh_shape
    ys = 4 if nx % 8 == 0 else 1
    zs = nx // (2 * ys)
    bodies, contacts = body_load.shape[3], contact_blocks.shape[4]
    chunks, tiles, spans = bodies // LANES, contacts // LANES, bodies // SPAN
    f32, bf16, i32 = jnp.float32, jnp.bfloat16, jnp.int32
    vmem = pltpu.VMEM
    dma = pltpu.SemaphoreType.DMA
    parts, wholes = ny * ys, 2 * zs - 1
    pair_rows = PAIR_ROWS * SPLITS
    operands = (
        body_load.reshape(FIELDS * chunks, LANES),
        proximal.reshape(FIELDS * chunks, LANES),
        contact_blocks.reshape(12 * FIELDS, tiles, LANES),
        slacks.reshape(FIELDS, tiles, LANES),
        dual_rows.reshape(FIELDS, tiles, LANES),
        first_body.reshape(tiles, LANES),
        second_body.reshape(tiles, LANES),
        border_bodies.reshape(border_bodies.shape[2:]),
    )
    scratch = [vmem(a.shape, a.dtype) for a in operands] + [
        dma((8,)),
        vmem((12 * FIELDS, tiles, LANES), f32),
        vmem((FIELDS * FIELDS, tiles, LANES), f32),
        vmem((contacts, SPAN), bf16),
        vmem((contacts, SPAN), bf16),
        vmem((2 * LANES, SPAN), bf16),
        vmem((tiles, ROWS, LANES), i32),
        vmem((tiles, ROWS, LANES), i32),
        vmem((2, ROWS, LANES), i32),
        vmem((2, ROWS, LANES), i32),
        vmem((2, ROWS, LANES), i32),
        vmem((ROWS, LANES), i32),
        vmem((pair_rows * spans, contacts), bf16),
        vmem((pair_rows * spans, contacts), bf16),
        vmem((pair_rows * HALO_SPANS + ROWS, contacts), bf16),
        vmem((pair_rows * spans, 2 * LANES), bf16),
        vmem((tiles * ROWS, LANES), f32),
        vmem((tiles * ROWS, LANES), f32),
        vmem((tiles * PAIR_ROWS, LANES), f32),
        vmem((tiles * PAIR_ROWS, LANES), f32),
        vmem((ITERS, chunks, ROWS, LANES), f32),
        vmem((ITERS + 1, chunks, ROWS, LANES), f32),
        vmem((chunks, ROWS, LANES), f32),
        vmem((FIELDS * chunks * ROWS, LANES), f32),
        vmem((chunks, PAIR_ROWS, LANES), f32),
        vmem((2, PAIR_ROWS, LANES), f32),
        vmem((FIELDS, 2, ROWS, LANES), f32),
        vmem((2, PAIR_ROWS, LANES), f32),
        vmem((8, PAIR_ROWS, LANES), f32),
        vmem((ITERS, 2, ROWS, LANES), f32),
        vmem((ITERS, 8, ROWS, LANES), f32),
        vmem((ITERS, 2, ROWS, LANES), f32),
        vmem((ITERS, 8, ROWS, LANES), f32),
        vmem((1, LANES), f32),
        vmem((parts, 1, LANES), f32),
        vmem((1, LANES), f32),
        vmem((wholes, 1, LANES), f32),
        vmem((1, LANES), f32),
        vmem((parts, 1, LANES), f32),
        vmem((1, LANES), f32),
        vmem((wholes, 1, LANES), f32),
        dma((8,)),
        dma((8,)),
        dma((ITERS, 8)),
        dma((ITERS, 8)),
        dma((ITERS, 8)),
        dma((ITERS, 8)),
        dma((parts,)),
        dma((parts,)),
        dma((wholes,)),
        dma((wholes,)),
        dma((parts,)),
        dma((parts,)),
        dma((wholes,)),
        dma((wholes,)),
    ]
    step, residual = pl.pallas_call(
        functools.partial(kernel, (nx, ny, ys, zs)),
        out_shape=[jax.ShapeDtypeStruct((2, FIELDS * chunks, LANES), f32)] * 2,
        in_specs=[pl.BlockSpec(memory_space=pltpu.HBM)] * 8,
        out_specs=[pl.BlockSpec(memory_space=pltpu.VMEM)] * 2,
        scratch_shapes=scratch,
        compiler_params=pltpu.CompilerParams(
            collective_id=0, has_side_effects=True, vmem_limit_bytes=32 * 1024 * 1024
        ),
    )(*[pltpu.with_memory_space_constraint(a, pltpu.HBM) for a in operands])
    step, residual = step[0] + step[1], residual[0] + residual[1]
    return step.reshape(body_load.shape), residual.reshape(body_load.shape)


def solution(mesh):
    return jax.shard_map(
        functools.partial(local, (mesh.shape["gx"], mesh.shape["gy"])),
        mesh=mesh,
        in_specs=(
            P("gx", "gy", None, None),
            P("gx", "gy", None, None),
            P("gx", "gy", None, None, None),
            P("gx", "gy", None, None),
            P("gx", "gy", None, None),
            P("gx", "gy", None),
            P("gx", "gy", None),
            P("gx", "gy", None, None),
        ),
        out_specs=(P("gx", "gy", None, None), P("gx", "gy", None, None)),
        check_vma=False,
    )
```

```python
import functools

import jax
import jax.numpy as jnp
from jax import lax
from jax.experimental import pallas as pl
from jax.experimental.pallas import tpu as pltpu
from jax.sharding import PartitionSpec as P

ITERS = 4
LANES = 128
ROWS = 8
SPAN = 256
HALO_SPANS = 2 * LANES // SPAN
SPLITS = 3
LOOP_SPLITS = 3
FIELDS = 6
PAIRS = [(a, b) for a in range(FIELDS) for b in range(a, FIELDS)]
PAIR_ROWS = 24
MESH = pl.DeviceIdType.MESH
OFFSETS = ((-1, -1), (-1, 0), (-1, 1), (0, -1), (0, 1), (1, -1), (1, 0), (1, 1))
FAR = (0, 2, 5, 7)
CLOSE = (1, 6, 3, 4)


def pick(source, lane):
    return jnp.take_along_axis(source, lane, axis=1, mode="promise_in_bounds")


def add_up(values):
    while len(values) > 1:
        pairs = [a + b for a, b in zip(values[::2], values[1::2])]
        values = pairs + values[len(pairs) * 2 :]
    return values[0]


def split_terms(values, splits):
    terms = []
    for number in range(splits):
        term = values.astype(jnp.bfloat16).astype(jnp.float32)
        terms.append(term)
        if number + 1 < splits:
            values = values - term
    return terms


def dot(left, hot):
    return lax.dot_general(
        left, hot, (((1,), (0,)), ((), ())), preferred_element_type=jnp.float32
    )


def sum_rows(values):
    for shift in (4, 2, 1):
        values = values + pltpu.roll(values, shift, 0)
    return values


def inverse_six(entry):
    lower, flipped = {}, []
    for column in range(6):
        scaled = [lower[column, inner] * flipped[inner][0] for inner in range(column)]
        value = entry(column, column)
        for inner in range(column):
            value = value - scaled[inner] * lower[column, inner]
        flipped.append((value, 1.0 / value))
        for row in range(column + 1, 6):
            value = entry(column, row)
            for inner in range(column):
                value = value - lower[row, inner] * scaled[inner]
            lower[row, column] = value * flipped[column][1]
    unit = {}
    for column in range(6):
        for row in range(column + 1, 6):
            value = -lower[row, column]
            for inner in range(column + 1, row):
                value = value - lower[row, inner] * unit[inner, column]
            unit[row, column] = value
    result = {}
    for row in range(6):
        weighted = {inner: flipped[inner][1] * unit[inner, row] for inner in range(row + 1, 6)}
        weighted[row] = flipped[row][1]
        for column in range(row + 1):
            terms = []
            for inner in range(row, 6):
                term = weighted[inner]
                terms.append(term if inner == column else term * unit[inner, column])
            result[row, column] = result[column, row] = add_up(terms)
    return result


def weigh(left, right, moments, skip=None):
    weights = {}
    for i, a in enumerate(left):
        for j, b in enumerate(right):
            if i + j != skip:
                weights.setdefault(i + j, []).append(a * b)
    return add_up([add_up(w) * moments[i] for i, w in weights.items()])


def image_of(direction):
    return [
        add_up([direction[i] for i in (j - 1, j) if 0 <= i < len(direction)])
        for j in range(len(direction) + 1)
    ]


def coefficients(moments):
    one = jnp.ones_like(moments[0])
    step, residual, direction = [], [one], [one]
    norm_now = moments[0]
    for iteration in range(ITERS - 1):
        image = image_of(direction)
        length = norm_now / weigh(direction, image, moments)
        step = [a + length * b for a, b in zip(step, direction)] + [length * direction[-1]]
        residual = [a - length * b for a, b in zip(residual, image)] + [-length * image[-1]]
        norm_next = weigh(residual, residual, moments)
        ratio = norm_next / norm_now
        direction = [a + ratio * b for a, b in zip(residual, direction)] + [residual[-1]]
        norm_now = norm_next
    return step, residual, direction, image_of(direction), norm_now


def energy_rest(direction, image, moments):
    top = len(direction) - 1
    rest = weigh(direction, image, moments, skip=2 * top + 1)
    return rest - direction[top] * image[top + 1] * moments[2 * top]


def kernel(
    sizes,
    load_hbm, prox_hbm, block_hbm, slack_hbm, dual_hbm, first_hbm, second_hbm, border_hbm,
    step_ref, residual_ref,
    load_in, prox_in, block_in, slack_in, dual_in, first_in, second_in, border_in, in_sem,
    g, cross, hot1, hot2, hotb, span1, span2, spanb, laneb, chunkb, border_pad,
    left1, left2, left_halo, leftb, spread, spread_first, spread_pairs, spread_pairs_first,
    basis_v, basis_q, prox, inverse, diag, returned, columns,
    diag_send, diag_recv, fore_send, fore_recv, back_send, back_recv,
    early_send, early_recv, early_whole_send, early_whole_recv,
    part_send, part_recv, whole_send, whole_recv,
    diag_ssem, diag_rsem, fore_ssem, fore_rsem, back_ssem, back_rsem,
    early_ssem, early_rsem, early_whole_ssem, early_whole_rsem,
    part_ssem, part_rsem, whole_ssem, whole_rsem,
):
    nx, ny, ys, zs = sizes
    chunks = load_hbm.shape[0] // FIELDS
    spans = chunks * LANES // SPAN
    tiles = first_in.shape[0]
    HALO = range(spans, spans + HALO_SPANS)
    f32, bf16 = jnp.float32, jnp.bfloat16
    gx, gy = lax.axis_index("gx"), lax.axis_index("gy")
    z_at, y_at, core = gx // (2 * ys), (gx // 2) % ys, gx % 2

    near = [((gx + dx + nx) % nx, (gy + dy + ny) % ny) for dx, dy in OFFSETS]
    real = []
    for dx, dy in OFFSETS:
        to_x, to_y = gx + dx, gy + dy
        real.append((to_x >= 0) & (to_x < nx) & (to_y >= 0) & (to_y < ny))
    part_count, whole_count = ny * ys, zs * 2
    part_near, whole_near = [], []
    for offset in range(part_count):
        other = (gy * ys + y_at + offset) % part_count
        part_near.append((z_at * 2 * ys + (other % ys) * 2 + 1 - core, other // ys))
    for offset in range(1, whole_count):
        other = (z_at * 2 + core + offset) % whole_count
        whole_near.append(((other // 2) * 2 * ys + y_at * 2 + other % 2, gy))
    barrier = pltpu.get_barrier_semaphore()
    everyone = [near[k] for k in FAR + CLOSE] + part_near + whole_near
    for device in everyone:
        pl.semaphore_signal(barrier, inc=1, device_id=device, device_id_type=MESH)

    loads = []
    for number, (source, target) in enumerate(
        (
            (second_hbm, second_in),
            (block_hbm, block_in),
            (slack_hbm, slack_in),
            (dual_hbm, dual_in),
            (first_hbm, first_in),
            (border_hbm, border_in),
            (load_hbm, load_in.at[0 : load_hbm.shape[0]]),
            (prox_hbm, prox_in.at[0 : prox_hbm.shape[0]]),
        )
    ):
        loads.append(pltpu.make_async_copy(source, target, in_sem.at[number]))
        loads[-1].start()

    lane_group = lax.broadcasted_iota(jnp.int32, (1, LANES), 1) // 32
    lane_at = lax.broadcasted_iota(jnp.int32, (LANES, LANES), 1)

    def build_hot(hot, row, at):
        spot = jnp.transpose(jnp.broadcast_to(row % SPAN, (LANES, LANES)).astype(f32))
        for part in range(SPAN // LANES):
            same = spot == (lane_at + part * LANES).astype(f32)
            hot[at : at + LANES, part * LANES : (part + 1) * LANES] = jnp.where(
                same, 1.0, 0.0
            ).astype(bf16)

    def write_terms(target, values, masks, splits):
        pieces = [jnp.where(mask, t, 0.0) for t in split_terms(values, splits) for mask in masks]
        if (len(pieces) * values.shape[1]) % 16:
            pieces.append(jnp.zeros((values.shape[0], ROWS, LANES), f32))
        packed = jnp.concatenate(pieces, axis=1).astype(bf16)
        for s in range(values.shape[0]):
            target[0 : packed.shape[1], s * LANES : (s + 1) * LANES] = packed[s]
        return packed.shape[1]

    def read_terms(product, rows, masks, splits):
        result = []
        for mask in range(masks):
            total = add_up(
                [
                    product[(n * masks + mask) * rows : (n * masks + mask + 1) * rows]
                    for n in range(splits)
                ]
            )
            result.extend([total[:, at : at + LANES] for at in range(0, SPAN, LANES)])
        return result

    def arrange(slots, place_of):
        halves = [[], []]
        for k in range(8):
            place = place_of(k)
            code = jnp.where(real[k], place % 4, -1)
            halves[place // 4].append(jnp.where(lane_group == code, slots(k), 0.0))
        return [add_up(half) for half in halves]

    def reverse(k):
        return 7 - k

    def forward(k):
        return k

    def exchange(send, recv, ssem, rsem, place_of, directions=FAR + CLOSE):
        copies = []
        for k in directions:
            copies.append(
                pltpu.make_async_remote_copy(
                    src_ref=send.at[place_of(k) // 4],
                    dst_ref=recv.at[7 - k],
                    send_sem=ssem.at[k],
                    recv_sem=rsem.at[7 - k],
                    device_id=near[k],
                    device_id_type=MESH,
                )
            )
            copies[-1].start()
        return copies

    def broadcast_all(sender, receiver, ssem, rsem, devices):
        copies = []
        for number, device in enumerate(devices):
            copies.append(
                pltpu.make_async_remote_copy(
                    src_ref=sender,
                    dst_ref=receiver.at[number],
                    send_sem=ssem.at[number],
                    recv_sem=rsem.at[number],
                    device_id=device,
                    device_id_type=MESH,
                )
            )
            copies[-1].start()
        return copies

    def sent(copies):
        for copy in copies:
            copy.wait_send()

    def arrived(copies):
        for copy in copies:
            copy.wait_recv()

    spread[...] = jnp.zeros_like(spread)
    spread_first[...] = jnp.zeros_like(spread_first)
    spread_pairs[...] = jnp.zeros_like(spread_pairs)
    spread_pairs_first[...] = jnp.zeros_like(spread_pairs_first)
    loads[0].wait()
    for s in range(tiles):
        row = second_in[s : s + 1, :]
        span2[s] = jnp.broadcast_to(row // SPAN, (ROWS, LANES))
        build_hot(hot2, row, s * LANES)

    def masks_of(span, rows, wanted):
        value = span[...]
        if rows != ROWS:
            value = jnp.concatenate([value] * (rows // ROWS), axis=1)
        return [value == number for number in wanted]

    def pair_products(base, target):
        for p, (a, b) in enumerate(PAIRS):
            value = add_up([g[r * 12 + base + a] * g[r * 12 + base + b] for r in range(6)])
            target[pl.ds(p, tiles, stride=PAIR_ROWS), :] = value

    for number in (1, 2, 3):
        loads[number].wait()
    root = [jnp.sqrt(dual_in[r] / slack_in[r]) for r in range(6)]
    for r in range(6):
        for j in range(6, 12):
            g[r * 12 + j] = block_in[r * 12 + j] * root[r]
    pair_products(6, spread_pairs)
    pair_values = spread_pairs[...].reshape(tiles, PAIR_ROWS, LANES)
    rows = write_terms(left_halo, pair_values, masks_of(span2, PAIR_ROWS, HALO), SPLITS)
    halves = read_terms(dot(left_halo[0:rows, :], hot2[...]), PAIR_ROWS, HALO_SPANS, SPLITS)
    for half in range(2):
        diag_send[half] = halves[half]
    pl.semaphore_wait(barrier, len(everyone))
    copies = exchange(diag_send, diag_recv, diag_ssem, diag_rsem, forward)

    rows = write_terms(left2, pair_values, masks_of(span2, PAIR_ROWS, range(spans)), SPLITS)
    local2 = read_terms(dot(left2[0:rows, :], hot2[...]), PAIR_ROWS, spans, SPLITS)
    for r in range(6):
        for j in range(6):
            g[r * 12 + j] = block_in[r * 12 + j] * root[r]
    pair_products(0, spread_pairs_first)
    loads[4].wait()
    for s in range(tiles):
        row = first_in[s : s + 1, :]
        span1[s] = jnp.broadcast_to(row // SPAN, (ROWS, LANES))
        build_hot(hot1, row, s * LANES)
    for j in range(6):
        for a in range(6):
            cross[j * 6 + a] = add_up([g[r * 12 + 6 + j] * g[r * 12 + a] for r in range(6)])
    pair_values = spread_pairs_first[...].reshape(tiles, PAIR_ROWS, LANES)
    rows = write_terms(left1, pair_values, masks_of(span1, PAIR_ROWS, range(spans)), SPLITS)
    local1 = read_terms(dot(left1[0:rows, :], hot1[...]), PAIR_ROWS, spans, SPLITS)
    for c in range(chunks):
        diag[c] = local1[c] + local2[c]
    loads[5].wait()
    border_pad[...] = jnp.zeros_like(border_pad)
    border_pad[:, : border_in.shape[1]] = border_in[...]
    for half in range(2):
        row = border_pad[7 - 4 * half : 8 - 4 * half, :]
        for quarter in range(1, 4):
            place = 4 * half + quarter
            moved = pltpu.roll(border_pad[7 - place : 8 - place, :], 32 * quarter, 1)
            row = jnp.where(lane_group == quarter, moved, row)
        build_hot(hotb, row, half * LANES)
        whole = jnp.broadcast_to(row, (ROWS, LANES))
        laneb[half] = whole % LANES
        chunkb[half] = whole // LANES
        spanb[half] = whole // SPAN
    loads[6].wait()
    loads[7].wait()
    zero_rows = jnp.zeros((ROWS - FIELDS, LANES), f32)
    for c in range(chunks):
        basis_q[0, c] = jnp.concatenate(
            [load_in[pl.ds(c, FIELDS, stride=chunks), :], zero_rows], axis=0
        )
        prox[c] = jnp.concatenate(
            [prox_in[pl.ds(c, FIELDS, stride=chunks), :], zero_rows], axis=0
        )
    inverse[...] = jnp.zeros_like(inverse)
    columns[...] = jnp.zeros_like(columns)
    lane1, chunk1 = first_in[...] % LANES, first_in[...] // LANES
    lane2, chunk2 = second_in[...] % LANES, second_in[...] // LANES

    sent(copies)
    arrived(copies)
    halves = arrange(lambda k: diag_recv[k], reverse)
    for half in range(2):
        returned[half] = halves[half]
    rows = write_terms(leftb, returned[...], masks_of(spanb, PAIR_ROWS, range(spans)), SPLITS)
    localb = read_terms(dot(leftb[0:rows, :], hotb[...]), PAIR_ROWS, spans, SPLITS)
    entries = {}
    for c in range(chunks):
        spread_pairs[pl.ds(c, PAIR_ROWS, stride=ROWS), :] = diag[c] + localb[c]
    for p, (a, b) in enumerate(PAIRS):
        value = spread_pairs[p * ROWS : p * ROWS + chunks, :]
        if a == b:
            value = value + prox_in[a * chunks : (a + 1) * chunks, :]
        entries[a, b] = value
    for (a, b), value in inverse_six(lambda a, b: entries[a, b]).items():
        inverse[pl.ds(b * chunks * ROWS + a, chunks, stride=ROWS), :] = value

    def precondition(field):
        result = []
        for c in range(chunks):
            terms = []
            for b in range(FIELDS):
                at = (b * chunks + c) * ROWS
                terms.append(
                    inverse[at : at + ROWS, :]
                    * jnp.broadcast_to(field[c][b : b + 1, :], (ROWS, LANES))
                )
            result.append(add_up(terms))
        return result

    moments = jnp.zeros((1, LANES), f32)
    moment_group = lax.broadcasted_iota(jnp.int32, (1, LANES), 1) // 16

    def inner(left, right):
        value = sum_rows(add_up([left[c] * right[c] for c in range(chunks)]))[0:1]
        for shift in (64, 32, 16):
            value = value + pltpu.roll(value, shift, 1)
        return value

    def gather_fields(rows_of, lane, chunk, start, count):
        result = []
        for f in range(FIELDS):
            value = None
            for n in range(count):
                source = jnp.broadcast_to(rows_of(f, n), (tiles, LANES))
                piece = pick(source, lane)
                if value is None:
                    value = piece if start == 0 else jnp.where(chunk == start, piece, 0.0)
                else:
                    value = jnp.where(chunk == start + n, piece, value)
            result.append(value)
        return result

    q_now = [basis_q[0, c] for c in range(chunks)]
    v_now = precondition(q_now)
    late = []
    for k in range(ITERS):
        for c in range(chunks):
            basis_v[k, c] = v_now[c]
        ends = []
        for half in range(2):
            value = pick(v_now[0], laneb[half])
            for c in range(1, chunks):
                value = jnp.where(chunkb[half] == c, pick(v_now[c], laneb[half]), value)
            ends.append(value)
            fore_send[k, half] = value
        fore_refs = (fore_send.at[k], fore_recv.at[k], fore_ssem.at[k], fore_rsem.at[k], reverse)
        back_refs = (back_send.at[k], back_recv.at[k], back_ssem.at[k], back_rsem.at[k], forward)
        fore = exchange(*fore_refs, FAR)
        u1 = gather_fields(lambda f, n: basis_v[k, n, f : f + 1, :], lane1, chunk1, 0, chunks)
        for j in range(6):
            value = add_up([cross[j * 6 + a] * u1[a] for a in range(6)])
            spread[pl.ds(j, tiles, stride=ROWS), :] = value
        pulls = spread[...].reshape(tiles, ROWS, LANES)
        rows = write_terms(left_halo, pulls, masks_of(span2, ROWS, HALO), LOOP_SPLITS)
        halves = read_terms(dot(left_halo[0:rows, :], hot2[...]), ROWS, HALO_SPANS, LOOP_SPLITS)
        for half in range(2):
            back_send[k, half] = halves[half]
        back = exchange(*back_refs, FAR)
        fore = fore + exchange(*fore_refs, CLOSE)
        back = back + exchange(*back_refs, CLOSE)
        norm = inner(v_now, q_now)
        moments = jnp.where(moment_group == 2 * k, norm, moments)
        if k == ITERS - 1:
            early_send[...] = moments
            early = broadcast_all(early_send, early_recv, early_ssem, early_rsem, part_near)
        u2 = gather_fields(lambda f, n: basis_v[k, n, f : f + 1, :], lane2, chunk2, 0, chunks)
        here = chunk2 < chunks
        u2 = [jnp.where(here, value, 0.0) for value in u2]
        strain = [
            add_up(
                [g[r * 12 + j] * u1[j] for j in range(6)]
                + [g[r * 12 + 6 + j] * u2[j] for j in range(6)]
            )
            for r in range(6)
        ]
        for j in range(6):
            value = add_up([g[r * 12 + 6 + j] * strain[r] for r in range(6)])
            spread[pl.ds(j, tiles, stride=ROWS), :] = value
        pulls = spread[...].reshape(tiles, ROWS, LANES)
        rows = write_terms(left2, pulls, masks_of(span2, ROWS, range(spans)), LOOP_SPLITS)
        image = read_terms(dot(left2[0:rows, :], hot2[...]), ROWS, spans, LOOP_SPLITS)
        image = [image[c] + prox[c] * v_now[c] - q_now[c] for c in range(chunks)]
        pushes = [add_up([g[r * 12 + j] * strain[r] for r in range(6)]) for j in range(6)]
        if k == 0:
            for p, (a, b) in enumerate(PAIRS):
                for half in range(2):
                    row = returned[half, p : p + 1, :]
                    columns[b, half, a : a + 1, :] = row
                    if a != b:
                        columns[a, half, b : b + 1, :] = row
        pulled = []
        for half in range(2):
            pulled.append(
                add_up(
                    [
                        columns[b, half]
                        * jnp.broadcast_to(ends[half][b : b + 1, :], (ROWS, LANES))
                        for b in range(FIELDS)
                    ]
                )
            )
        sent(late)
        sent(fore)
        arrived(fore)
        beyond = arrange(lambda s: fore_recv[k, s], forward)
        u2 = gather_fields(lambda f, n: beyond[n][f : f + 1, :], lane2, chunk2, chunks, 2)
        for a in range(6):
            value = pushes[a] + add_up([cross[j * 6 + a] * u2[j] for j in range(6)])
            spread_first[pl.ds(a, tiles, stride=ROWS), :] = value
        if k == ITERS - 1:
            more = [add_up([g[r * 12 + 6 + j] * u2[j] for j in range(6)]) for r in range(6)]
            energy = add_up([(strain[r] + more[r]) * (strain[r] + more[r]) for r in range(6)])
            energy = add_up([energy[t : t + ROWS] for t in range(0, tiles, ROWS)])
            energy = energy + add_up([prox[c] * v_now[c] * v_now[c] for c in range(chunks)])
            part_send[...] = sum_rows(energy)[0:1]
            part = broadcast_all(part_send, part_recv, part_ssem, part_rsem, part_near)
        values = spread_first[...].reshape(tiles, ROWS, LANES)
        rows = write_terms(left1, values, masks_of(span1, ROWS, range(spans)), LOOP_SPLITS)
        pushed = read_terms(dot(left1[0:rows, :], hot1[...]), ROWS, spans, LOOP_SPLITS)
        image = [image[c] + pushed[c] for c in range(chunks)]
        arrived(back)
        late = back
        halves = arrange(lambda s: back_recv[k, s], reverse)
        values = jnp.concatenate([(halves[h] + pulled[h])[None] for h in range(2)], axis=0)
        rows = write_terms(leftb, values, masks_of(spanb, ROWS, range(spans)), LOOP_SPLITS)
        added = read_terms(dot(leftb[0:rows, :], hotb[...]), ROWS, spans, LOOP_SPLITS)
        q_next = [image[c] + added[c] for c in range(chunks)]
        for c in range(chunks):
            basis_q[k + 1, c] = q_next[c]
        if k < ITERS - 1:
            v_next = precondition(q_next)
            moments = jnp.where(moment_group == 2 * k + 1, inner(v_now, q_next), moments)
            q_now, v_now = q_next, v_next

    sent(early)
    arrived(early)
    early_whole_send[...] = add_up([early_recv[n] for n in range(len(part_near))])
    early = broadcast_all(
        early_whole_send, early_whole_recv, early_whole_ssem, early_whole_rsem, whole_near
    )
    sent(late)
    sent(part)
    arrived(part)
    whole_send[...] = add_up([part_recv[n] for n in range(len(part_near))])
    whole = broadcast_all(whole_send, whole_recv, whole_ssem, whole_rsem, whole_near)
    sent(early)
    arrived(early)
    total = early_whole_send[...] + add_up([early_whole_recv[n] for n in range(len(whole_near))])
    row_at = lax.broadcasted_iota(jnp.int32, (ROWS, LANES), 0)
    group_at = lax.broadcasted_iota(jnp.int32, (ROWS, LANES), 1) // 16
    total = jnp.where(row_at == group_at, jnp.broadcast_to(total, (ROWS, LANES)), 0.0)
    sums = jnp.sum(total, axis=1, keepdims=True)
    moments = [jnp.broadcast_to(sums[i : i + 1, :], (ROWS, LANES)) for i in range(2 * ITERS - 1)]
    step, residual, direction, image, norm_now = coefficients(moments)
    rest = energy_rest(direction, image, moments)
    before, ahead, left, drop = [], [], [], []
    for c in range(chunks):
        before.append(add_up([step[j] * basis_v[j, c] for j in range(ITERS - 1)]))
        ahead.append(add_up([direction[j] * basis_v[j, c] for j in range(ITERS)]))
        left.append(add_up([residual[j] * basis_q[j, c] for j in range(ITERS)]))
        drop.append(add_up([image[j] * basis_q[j, c] for j in range(ITERS + 1)]))
    sent(whole)
    arrived(whole)
    total = whole_send[...] + add_up([whole_recv[n] for n in range(len(whole_near))])
    energy = jnp.broadcast_to(jnp.sum(total, axis=1, keepdims=True), (ROWS, LANES))
    length = norm_now / (rest + direction[-1] * image[-1] * energy)
    for c in range(chunks):
        rows = pl.ds(c, FIELDS, stride=chunks)
        step_ref[0, rows, :] = before[c][0:FIELDS]
        step_ref[1, rows, :] = (length * ahead[c])[0:FIELDS]
        residual_ref[0, rows, :] = left[c][0:FIELDS]
        residual_ref[1, rows, :] = (-length * drop[c])[0:FIELDS]


def local(mesh_shape, body_load, proximal, contact_blocks, slacks, dual_rows, first_body, second_body, border_bodies):
    nx, ny = mesh_shape
    ys = 4 if nx % 8 == 0 else 1
    zs = nx // (2 * ys)
    bodies, contacts = body_load.shape[3], contact_blocks.shape[4]
    chunks, tiles, spans = bodies // LANES, contacts // LANES, bodies // SPAN
    f32, bf16, i32 = jnp.float32, jnp.bfloat16, jnp.int32
    vmem = pltpu.VMEM
    dma = pltpu.SemaphoreType.DMA
    parts, wholes = ny * ys, 2 * zs - 1
    pair_rows = PAIR_ROWS * SPLITS
    operands = (
        body_load.reshape(FIELDS * chunks, LANES),
        proximal.reshape(FIELDS * chunks, LANES),
        contact_blocks.reshape(12 * FIELDS, tiles, LANES),
        slacks.reshape(FIELDS, tiles, LANES),
        dual_rows.reshape(FIELDS, tiles, LANES),
        first_body.reshape(tiles, LANES),
        second_body.reshape(tiles, LANES),
        border_bodies.reshape(border_bodies.shape[2:]),
    )
    field_rows = ROWS * chunks
    scratch = [vmem((field_rows, LANES), f32)] * 2
    scratch += [vmem(a.shape, a.dtype) for a in operands[2:]] + [
        dma((8,)),
        vmem((12 * FIELDS, tiles, LANES), f32),
        vmem((FIELDS * FIELDS, tiles, LANES), f32),
        vmem((contacts, SPAN), bf16),
        vmem((contacts, SPAN), bf16),
        vmem((2 * LANES, SPAN), bf16),
        vmem((tiles, ROWS, LANES), i32),
        vmem((tiles, ROWS, LANES), i32),
        vmem((2, ROWS, LANES), i32),
        vmem((2, ROWS, LANES), i32),
        vmem((2, ROWS, LANES), i32),
        vmem((ROWS, LANES), i32),
        vmem((pair_rows * spans, contacts), bf16),
        vmem((pair_rows * spans, contacts), bf16),
        vmem((pair_rows * HALO_SPANS + ROWS, contacts), bf16),
        vmem((pair_rows * spans, 2 * LANES), bf16),
        vmem((tiles * ROWS, LANES), f32),
        vmem((tiles * ROWS, LANES), f32),
        vmem((tiles * PAIR_ROWS, LANES), f32),
        vmem((tiles * PAIR_ROWS, LANES), f32),
        vmem((ITERS, chunks, ROWS, LANES), f32),
        vmem((ITERS + 1, chunks, ROWS, LANES), f32),
        vmem((chunks, ROWS, LANES), f32),
        vmem((FIELDS * chunks * ROWS + 8 * ROWS, LANES), f32),
        vmem((chunks, PAIR_ROWS, LANES), f32),
        vmem((2, PAIR_ROWS, LANES), f32),
        vmem((FIELDS, 2, ROWS, LANES), f32),
        vmem((2, PAIR_ROWS, LANES), f32),
        vmem((8, PAIR_ROWS, LANES), f32),
        vmem((ITERS, 2, ROWS, LANES), f32),
        vmem((ITERS, 8, ROWS, LANES), f32),
        vmem((ITERS, 2, ROWS, LANES), f32),
        vmem((ITERS, 8, ROWS, LANES), f32),
        vmem((1, LANES), f32),
        vmem((parts, 1, LANES), f32),
        vmem((1, LANES), f32),
        vmem((wholes, 1, LANES), f32),
        vmem((1, LANES), f32),
        vmem((parts, 1, LANES), f32),
        vmem((1, LANES), f32),
        vmem((wholes, 1, LANES), f32),
        dma((8,)),
        dma((8,)),
        dma((ITERS, 8)),
        dma((ITERS, 8)),
        dma((ITERS, 8)),
        dma((ITERS, 8)),
        dma((parts,)),
        dma((parts,)),
        dma((wholes,)),
        dma((wholes,)),
        dma((parts,)),
        dma((parts,)),
        dma((wholes,)),
        dma((wholes,)),
    ]
    step, residual = pl.pallas_call(
        functools.partial(kernel, (nx, ny, ys, zs)),
        out_shape=[jax.ShapeDtypeStruct((2, field_rows, LANES), f32)] * 2,
        in_specs=[pl.BlockSpec(memory_space=pltpu.HBM)] * 8,
        out_specs=[pl.BlockSpec(memory_space=pltpu.VMEM)] * 2,
        scratch_shapes=scratch,
        compiler_params=pltpu.CompilerParams(
            collective_id=0, has_side_effects=True, vmem_limit_bytes=32 * 1024 * 1024
        ),
    )(*[pltpu.with_memory_space_constraint(a, pltpu.HBM) for a in operands])
    step, residual = step[:, : FIELDS * chunks], residual[:, : FIELDS * chunks]
    step, residual = step[0] + step[1], residual[0] + residual[1]
    return step.reshape(body_load.shape), residual.reshape(body_load.shape)


def solution(mesh):
    return jax.shard_map(
        functools.partial(local, (mesh.shape["gx"], mesh.shape["gy"])),
        mesh=mesh,
        in_specs=(
            P("gx", "gy", None, None),
            P("gx", "gy", None, None),
            P("gx", "gy", None, None, None),
            P("gx", "gy", None, None),
            P("gx", "gy", None, None),
            P("gx", "gy", None),
            P("gx", "gy", None),
            P("gx", "gy", None, None),
        ),
        out_specs=(P("gx", "gy", None, None), P("gx", "gy", None, None)),
        check_vma=False,
    )
```
